512 devices in a mesh: grp: 16 (over y_hi, x, core), blk: 32 (over y_lo, z).
Axes of the slice: x: 4, y: 4 (y_hi: 2, y_lo: 2; y = y_hi * 2 + y_lo), z: 16, core: 2. Of those that a mesh axis runs over, the one named last changes fastest.
Arguments:
- video_encoder_output: bfloat16 [65536, 1024], P(('grp', 'blk')), may hold values from -3 to 3
- caption_encoder_output: bfloat16 [65536, 1024], P(('grp', 'blk')), may hold values from -3 to 3
- video_map_matrix: bfloat16 [1024, 1024], replicated, may hold values from -0.1875 to 0.1875
- caption_map_matrix: bfloat16 [1024, 1024], replicated, may hold values from -0.1875 to 0.1875
- matching_caption: int32 [65536], P('grp'), may hold values from 0 to 4095
- score_multiplier: float32 [1], replicated, may hold values from 32 to 64
- score_offset: float32 [1], replicated, may hold values from -5 to -3
Outputs:
- clip_hidden_grad: bfloat16 [65536, 1024], P(('grp', 'blk'))
- text_hidden_grad: bfloat16 [65536, 1024], P(('grp', 'blk'))
- clip_weight_grad: float32 [1024, 1024], P('blk')
- text_weight_grad: float32 [1024, 1024], P('blk')
The draws below stay inside these ranges and needn't reach their ends.
Inputs may be any that keep to these rules, and one draw needn't show every extreme that they name: `matching_caption`: each entry indexes the positive commentary of that clip within the clip's own group of 4096 pairs, counted from 0 in that group; several clips may share one commentary, and some commentaries are the positive of no clip.
All inputs are finite; a program needn't handle non-finite values.
Results may differ from the reference program's by a relative error of at most 0.015.
Values may be sent and summed in bfloat16 or wider, within the bound.
A program may use at most 64 MiB of HBM per device.

```python
import jax
import jax.numpy as jnp
from jax import lax

D = 1024
E = 1024
TOK_DEV = 128
GROUP = 4096
TOKENS = 65536


def touch_ends(array, rng, smallest, top_value):
    longest = array.shape.index(max(array.shape))
    spots = []
    for shift in (0, 1):
        where = [jax.random.randint(jax.random.fold_in(rng, axis), (), 0, length) for axis, length in enumerate(array.shape)]
        where[longest] = (where[longest] + shift) % array.shape[longest]
        spots.append(tuple(where))
    return array.at[spots[0]].set(smallest).at[spots[1]].set(top_value)


def spiked(drawn, own_key, source, target, parts, factor):
    def block_of(dim):
        return (jnp.arange(drawn.shape[dim]) // (drawn.shape[dim] // parts)).reshape((-1,) + (1,) * (drawn.ndim - 1 - dim))

    one_side = jax.random.permutation(own_key, parts)[block_of(target)]
    far = (block_of(target) + parts // 2) % parts
    return jnp.where((block_of(source) == one_side) | (block_of(source) == far), factor * drawn, drawn)


def levels(own_key, shape, shards, least, largest):
    factor_of = 1.0
    for position, parts in shards:
        draws = jax.random.uniform(jax.random.fold_in(jax.random.fold_in(own_key, 6), position), (parts,), jnp.float32, least / len(shards), largest / len(shards))
        factor_of = factor_of * jnp.repeat(jnp.exp(draws), shape[position] // parts).reshape((-1,) + (1,) * (len(shape) - 1 - position))
    return factor_of


def bell_draw(own_key, dims, width, limit, cuts=(), kind=jnp.bfloat16):
    level = levels(own_key, dims, cuts, -0.22, 0.18) if cuts else 1.0
    drawn = jax.random.normal(own_key, dims, jnp.float32) * width * level
    return jnp.minimum(jnp.maximum(drawn, -limit), limit).astype(kind)


def gaussian_with(own_key, extent, width, bound, split, heavy, held_as=jnp.bfloat16):
    values = width * jax.random.normal(own_key, extent, jnp.float32)
    if split:
        values = values * levels(own_key, extent, split, -0.22, 0.18)
    return jnp.clip(spiked(values, jax.random.fold_in(own_key, 3), *heavy), -bound, bound).astype(held_as)


def setup_inputs(seed: int = 0) -> dict:
    key_list = jax.random.split(jax.random.key(seed), 8)
    video_encoder_output = gaussian_with(key_list[0], (TOKENS, D), 0.125, 3.0, ((0, 512),), (0, 1, 512, 6.0))
    caption_encoder_output = gaussian_with(key_list[1], (TOKENS, D), 0.125, 3.0, ((0, 512),), (0, 1, 512, 6.0))
    video_map_matrix = bell_draw(key_list[2], (D, E), D ** -0.5, 0.1875)
    caption_map_matrix = bell_draw(key_list[3], (D, E), D ** -0.5, 0.1875)
    matching_caption = touch_ends(jax.random.randint(key_list[4], (TOKENS,), 0, GROUP), jax.random.fold_in(key_list[4], 1), 0, GROUP - 1).astype(jnp.int32)
    score_multiplier = jnp.clip(jax.random.uniform(key_list[5], (1,), jnp.float32, 32.0, 64.0), 32.0, 64.0)
    score_offset = jnp.clip(jax.random.uniform(key_list[6], (1,), jnp.float32, -5.0, -3.0), -5.0, -3.0)
    return {"video_encoder_output": video_encoder_output, "caption_encoder_output": caption_encoder_output, "video_map_matrix": video_map_matrix, "caption_map_matrix": caption_map_matrix, "matching_caption": matching_caption, "score_multiplier": score_multiplier, "score_offset": score_offset}


def project(hidden, weight):
    raw_value = jnp.dot(hidden, weight, preferred_element_type=jnp.float32)
    length = jnp.sqrt(lax.optimization_barrier(jnp.sum(raw_value * raw_value, axis=1, keepdims=True)) + 1e-06)
    return (length, raw_value / length)

def project_back(emb_grad, length, unit_vec):
    radial = lax.optimization_barrier(jnp.sum(unit_vec * emb_grad, axis=1, keepdims=True))
    return ((emb_grad - unit_vec * radial) / length).astype(jnp.bfloat16)

def device_terms(hidden, raw_grad):
    hidden_blocks = hidden.reshape(TOKENS // TOK_DEV, TOK_DEV, D)
    grad_blocks = raw_grad.reshape(TOKENS // TOK_DEV, TOK_DEV, E)

    def add_term(running, factor_inputs):
        device_term = jnp.dot(factor_inputs[0].T, factor_inputs[1], preferred_element_type=jnp.float32)
        rounded = lax.optimization_barrier(device_term.astype(jnp.bfloat16))
        return (running + rounded.astype(jnp.float32), None)
    running, unused = lax.scan(add_term, jnp.zeros((D, E), jnp.float32), (hidden_blocks, grad_blocks))
    return running

def batch_derivatives(video_batch, caption_batch, match_batch_index, score_scaled, shift_amount):
    pair_scores = score_scaled * jnp.dot(video_batch, caption_batch.T, preferred_element_type=jnp.float32) + shift_amount
    columns = jnp.arange(GROUP, dtype=jnp.int32)
    match_polarity = jnp.where(match_batch_index[:, None] == columns[None, :], 1.0, -1.0).astype(jnp.float32)
    match_factor = (-match_polarity * jax.nn.sigmoid(-match_polarity * pair_scores) * score_scaled).astype(jnp.bfloat16)
    clip_grad = jnp.dot(match_factor, caption_batch, preferred_element_type=jnp.float32)
    text_grad = jnp.dot(match_factor.T, video_batch, preferred_element_type=jnp.float32)
    return (clip_grad, text_grad)

def reference(video_encoder_output, caption_encoder_output, video_map_matrix, caption_map_matrix, matching_caption, score_multiplier, score_offset):
    score_scaled = score_multiplier[0]
    shift_amount = score_offset[0]
    clip_length, clip_unit = project(video_encoder_output, video_map_matrix)
    text_length, text_unit = project(caption_encoder_output, caption_map_matrix)
    video_vector = clip_unit.astype(jnp.bfloat16)
    caption_vector = text_unit.astype(jnp.bfloat16)
    group_count = TOKENS // GROUP

    def per_group(factor_inputs):
        return batch_derivatives(factor_inputs[0], factor_inputs[1], factor_inputs[2], score_scaled, shift_amount)
    clip_egrad, text_egrad = lax.map(per_group, (video_vector.reshape(group_count, GROUP, E), caption_vector.reshape(group_count, GROUP, E), matching_caption.reshape(group_count, GROUP)))
    clip_rgrad = project_back(clip_egrad.reshape(TOKENS, E), clip_length, clip_unit)
    text_rgrad = project_back(text_egrad.reshape(TOKENS, E), text_length, text_unit)
    clip_hgrad = jnp.dot(clip_rgrad, video_map_matrix.T, preferred_element_type=jnp.float32).astype(jnp.bfloat16)
    text_hgrad = jnp.dot(text_rgrad, caption_map_matrix.T, preferred_element_type=jnp.float32).astype(jnp.bfloat16)
    clip_wgrad = device_terms(video_encoder_output, clip_rgrad)
    text_weight_gradient = device_terms(caption_encoder_output, text_rgrad)
    return (clip_hgrad, text_hgrad, clip_wgrad, text_weight_gradient)
```

```python
import jax
import jax.numpy as jnp
from jax import lax
from jax.experimental import pallas as pl
from jax.experimental.pallas import tpu as pltpu
from jax.sharding import PartitionSpec as P

MESH = pl.DeviceIdType.MESH
F32 = jnp.float32
BF16 = jnp.bfloat16
NX, NZ, TOK, D, E = 4, 16, 128, 1024, 1024
HALF = TOK // 2
CLIP, TEXT = 0, 1


def kernel(
    hv_hbm,
    hc_hbm,
    wv_hbm,
    wc_hbm,
    match_ref,
    scale_ref,
    shift_ref,
    clip_hid,
    text_hid,
    clip_wg,
    text_wg,
    w,
    hx,
    ht,
    unit,
    length,
    tt,
    emb,
    part,
    cacc,
    back_in,
    back_out,
    share_out,
    share_in,
    g_out,
    g_in,
    y_out,
    y_in,
    z_out,
    z_in,
    f_all,
    load_sem,
    ring_s,
    ring_r,
    back_s,
    back_r,
    share_s,
    share_r,
    hid_s,
    hid_r,
    rel_s,
    rel_r,
    ga_s,
    ga_r,
    yb_s,
    yb_r,
    zc_s,
    zc_r,
    fd_s,
    fd_r,
):
    grp = lax.axis_index("grp")
    blk = lax.axis_index("blk")
    yh, x, core = grp // 8, (grp // 2) % 4, grp % 2
    yl, z = blk // NZ, blk % NZ
    y = yh * 2 + yl
    q = x * 2 + core

    def place(x=x, y=y, z=z, core=core):
        return ((y // 2) * 8 + x * 2 + core, (y % 2) * NZ + z)

    right, left = place(z=(z + 1) % NZ), place(z=(z + NZ - 1) % NZ)
    partner = place(y=yh * 2 + 1 - yl)
    sibling = place(core=1 - core)

    def remote(src, dst, s, r, device):
        return pltpu.make_async_remote_copy(
            src_ref=src, dst_ref=dst, send_sem=s, recv_sem=r, device_id=device, device_id_type=MESH
        )

    loads = [
        pltpu.make_async_copy(wc_hbm, w.at[TEXT], load_sem.at[0]),
        pltpu.make_async_copy(hc_hbm, hx.at[TEXT, q], load_sem.at[1]),
        pltpu.make_async_copy(wv_hbm, w.at[CLIP], load_sem.at[2]),
        pltpu.make_async_copy(hv_hbm, hx.at[CLIP, q], load_sem.at[3]),
    ]
    for copy in loads:
        copy.start()

    barrier = pltpu.get_barrier_semaphore()

    @pl.loop(1, NZ)
    def _(o):
        pl.semaphore_signal(barrier, 1, device_id=place(z=(z + o) % NZ), device_id_type=MESH)
        pl.semaphore_signal(barrier, 1, device_id=((grp + o) % 16, blk), device_id_type=MESH)

    pl.semaphore_signal(barrier, 1, device_id=place(y=(y + 1) % 4), device_id_type=MESH)
    pl.semaphore_signal(barrier, 1, device_id=place(y=(y + 3) % 4), device_id_type=MESH)

    def project(tower):
        raw = jnp.dot(hx[tower, q], w[tower], preferred_element_type=F32)
        size = jnp.sqrt(jnp.sum(raw * raw, axis=1, keepdims=True) + 1e-06)
        vec = raw / size
        unit[tower] = vec
        length[tower] = size
        return vec.astype(BF16)

    def ring(d, k, c):
        src = tt.at[k - 1, pl.ds((0 if isinstance(k, int) and k == 1 else TOK * d) + HALF * c, HALF)]
        dst = tt.at[k, pl.ds((0 if isinstance(k, int) and k == 8 else TOK * d) + HALF * c, HALF)]
        return remote(src, dst, ring_s.at[d, k - 1, c], ring_r.at[d, k - 1, c], (right, left)[d])

    def back(d, k, c):
        rows = pl.ds(HALF * c, HALF)
        return remote(
            back_out.at[d, k - 1, rows],
            back_in.at[d, k - 1, rows],
            back_s.at[d, k - 1, c],
            back_r.at[d, k - 1, c],
            (left, right)[d],
        )

    def hid_copy(tower, o, wait=False):
        index = ((x - o + 4) % 4) * 2 + core if wait else q
        return remote(
            hx.at[tower, index],
            hx.at[tower, index],
            hid_s.at[tower, o - 1],
            hid_r.at[tower, o - 1],
            place(x=(x + o) % NX),
        )

    def relay(tower, o, wait=False):
        index = ((x - o + 4) % 4) * 2 + ((1 - core) if wait else core)
        return remote(
            hx.at[tower, index], hx.at[tower, index], rel_s.at[tower, o], rel_r.at[tower, o], sibling
        )

    loads[0].wait()
    loads[1].wait()
    tt[0, pl.ds(0, TOK)] = project(TEXT)
    pl.semaphore_wait(barrier, 32)
    for c in (0, 1):
        ring(0, 1, c).start()
        ring(1, 1, 1 - c).start()
    loads[2].wait()
    loads[3].wait()
    emb[pl.ds(0, TOK)] = project(CLIP)
    share_emb = remote(
        emb.at[pl.ds(0, TOK)], emb.at[pl.ds(TOK, TOK)], share_s.at[0], share_r.at[0], partner
    )
    share_emb.start()
    for tower in (CLIP, TEXT):
        for o in (1, 3, 2):
            hid_copy(tower, o).start()
        relay(tower, 0).start()

    scale = scale_ref[0]
    shift = shift_ref[0]

    def work(k, rows):
        base0 = (yl * NZ + (z - k + NZ) % NZ) * TOK
        base1 = (yl * NZ + (z + k) % NZ) * TOK
        t = tt[k, pl.ds(0, rows)]
        a = emb[...]
        scores = scale * lax.dot_general(
            t, a, (((1,), (1,)), ((), ())), preferred_element_type=F32
        ) + shift
        row = lax.broadcasted_iota(jnp.int32, (rows, 2 * TOK), 0)
        place_of = jnp.where(row < TOK, base0 + row, base1 + row - TOK)
        wanted = jnp.concatenate(
            [match_ref[pl.ds(blk, 1), :], match_ref[pl.ds((1 - yl) * NZ + z, 1), :]], axis=1
        )
        hit = place_of == wanted
        flipped = jnp.where(hit, scores, -scores)
        coef = (jnp.where(hit, -scale, scale) / (1.0 + jnp.exp(flipped))).astype(BF16)
        part[k, pl.ds(0, rows)] = jnp.dot(coef, a, preferred_element_type=F32)
        return lax.dot_general(coef, t, (((0,), (0,)), ((), ())), preferred_element_type=F32)

    share_emb.wait_recv()
    cacc[...] = work(0, TOK)

    @pl.loop(1, 7)
    def _(k):
        for c in (0, 1):
            for d in (0, 1):
                cc = c if d == 0 else 1 - c
                ring_k(ring, d, k, cc)
        cacc[...] += work(k, 2 * TOK)

    def last_wait(d, k, c):
        ring(d, k, c).wait_recv()

    for d in (0, 1):
        last_wait(d, 7, d)
        ring(d, 8, d).start()
    for d in (0, 1):
        last_wait(d, 7, 1 - d)
    cacc[...] += work(7, 2 * TOK)

    def run(d, k, c):
        return part[k, pl.ds((0 if k == 8 else TOK * d) + HALF * c, HALF)]

    def send_fresh(d, k, c):
        back_out[d, k - 1, pl.ds(HALF * c, HALF)] = run(d, k, c).astype(BF16)
        back(d, k, c).start()

    def send_sum(d, k, c):
        rows = pl.ds(HALF * c, HALF)
        back(d, k + 1, c).wait_recv()
        back_out[d, k - 1, rows] = (run(d, k, c) + back_in[d, k, rows].astype(F32)).astype(BF16)
        back(d, k, c).start()

    for d in (0, 1):
        send_fresh(d, 7, 1 - d)
    for d in (0, 1):
        last_wait(d, 8, d)
    cacc[...] += work(8, TOK)
    for d in (0, 1):
        send_fresh(d, 8, d)

    share_out[...] = cacc[pl.ds(TOK, TOK)].astype(BF16)
    share_grad = remote(share_out, share_in, share_s.at[1], share_r.at[1], partner)
    share_grad.start()

    def ga_copy(tower, o, wait=False):
        to = (q + o) % 8
        slot = (q - o + 8) % 8 if wait else q
        return remote(
            g_out.at[tower, to],
            g_in.at[tower, slot],
            ga_s.at[tower, o - 1],
            ga_r.at[tower, o - 1],
            place(x=to // 2, core=to % 2),
        )

    def yb_copy(tower, o):
        to = (y + o) % 4
        return remote(
            y_out.at[tower, to],
            y_in.at[tower, o],
            yb_s.at[tower, o - 1],
            yb_r.at[tower, o - 1],
            place(y=to),
        )

    def zc_copy(tower, o):
        to = (z + o) % NZ
        return remote(
            z_out.at[tower, to],
            z_in.at[tower, o],
            zc_s.at[tower, o - 1],
            zc_r.at[tower, o - 1],
            place(z=to),
        )

    def fd_copy(tower, o, wait=False):
        to = (grp + o) % 16
        slot = (grp - o + 16) % 16 if wait else grp
        return remote(
            f_all.at[tower, slot if wait else grp],
            f_all.at[tower, slot],
            fd_s.at[tower, o - 1],
            fd_r.at[tower, o - 1],
            (to, blk),
        )

    def raw_grad(tower, grad):
        vec = unit[tower]
        radial = jnp.sum(vec * grad, axis=1, keepdims=True)
        raw = ((grad - vec * radial) / length[tower]).astype(BF16)
        for j in range(8):
            g_out[tower, j] = raw[:, 128 * j : 128 * (j + 1)]

        @pl.loop(1, 8)
        def _(o):
            ga_copy(tower, o).start()

        return raw

    def hidden_grad(tower, raw, out):
        out[...] = lax.dot_general(
            raw, w[tower], (((1,), (1,)), ((), ())), preferred_element_type=F32
        ).astype(BF16)

    def turn(tower, first, count):
        for j in range(first, first + count):
            ht[tower, :, pl.ds(128 * j, 128)] = hx[tower, j].T

    def weight(tower):
        g_in[tower, q] = g_out[tower, q]

        @pl.loop(1, 8)
        def _(o):
            ga_copy(tower, o, True).wait_recv()

        g = g_in[tower].reshape(8 * TOK, 128)
        for yl_to in (0, 1):
            term = jnp.dot(
                ht[tower, pl.ds(512 * yl_to, 512), :], g, preferred_element_type=F32
            ).reshape(NZ, 2, 16, 128).astype(BF16)
            for yh_to in (0, 1):
                y_out[tower, yh_to * 2 + yl_to] = term[:, yh_to]

        @pl.loop(1, 4)
        def _(o):
            yb_copy(tower, o).start()

    def over_y(tower):
        total = y_out[tower, y].astype(F32)
        for o in range(1, 4):
            yb_copy(tower, o).wait_recv()
            total = total + y_in[tower, o].astype(F32)
        z_out[tower] = total.astype(BF16)

        @pl.loop(1, NZ)
        def _(o):
            zc_copy(tower, o).start()

    def over_z(tower):
        @pl.loop(1, NZ)
        def _(o):
            zc_copy(tower, o).wait_recv()

        z_in[tower, 0] = z_out[tower, z]
        f_all[tower, grp] = jnp.sum(z_in[tower].astype(F32), axis=0)

        @pl.loop(1, 16)
        def _(o):
            fd_copy(tower, o).start()

    def finish(tower, out):
        @pl.loop(1, 16)
        def _(o):
            fd_copy(tower, o, True).wait_recv()

        for yh_from in (0, 1):
            for j in range(8):
                out[pl.ds(16 * yh_from, 16), pl.ds(128 * j, 128)] = f_all[tower, 8 * yh_from + j]

    def relays(tower):
        for o in (1, 2, 3):
            hid_copy(tower, o, True).wait_recv()
            relay(tower, o).start()

    def relays_done(tower):
        for o in range(4):
            relay(tower, o, True).wait_recv()

    def clip_back():
        share_grad.wait_recv()
        grad = cacc[pl.ds(0, TOK)] + share_in[...].astype(F32)
        hidden_grad(CLIP, raw_grad(CLIP, grad), clip_hid)

    def stage(j):
        if j == 6:
            relays(CLIP)
        elif j == 5:
            relays_done(CLIP)
            clip_back()
        elif j == 4:
            turn(CLIP, 0, 8)
        elif j == 3:
            weight(CLIP)
            relays(TEXT)
        elif j == 2:
            over_y(CLIP)
            relays_done(TEXT)
            turn(TEXT, 0, 4)
        elif j == 1:
            over_z(CLIP)
            turn(TEXT, 4, 4)
        else:
            finish(CLIP, clip_wg)

    for j in range(6, -1, -1):
        for d in (0, 1):
            if j >= 1:
                send_sum(d, j, 1 - d)
            else:
                back(d, 1, 1 - d).wait_recv()
        for d in (0, 1):
            send_sum(d, j + 1, d)
        stage(j)
    for d in (0, 1):
        back(d, 1, d).wait_recv()

    grad = part[0, pl.ds(0, TOK)] + back_in[0, 0].astype(F32) + back_in[1, 0].astype(F32)
    raw = raw_grad(TEXT, grad)
    hidden_grad(TEXT, raw, text_hid)
    weight(TEXT)
    over_y(TEXT)
    over_z(TEXT)
    finish(TEXT, text_wg)

    share_emb.wait_send()
    share_grad.wait_send()
    for d in (0, 1):
        for c in (0, 1):
            ring(d, 1, c).wait_send()

            @pl.loop(2, 8)
            def _(k):
                ring(d, k, c).wait_send()

            @pl.loop(1, 8)
            def _(k):
                back(d, k, c).wait_send()

        ring(d, 8, d).wait_send()
        back(d, 8, d).wait_send()
    for tower in (CLIP, TEXT):
        for o in range(4):
            relay(tower, o).wait_send()
        for o in (1, 2, 3):
            hid_copy(tower, o).wait_send()
            yb_copy(tower, o).wait_send()

        @pl.loop(1, 8)
        def _(o):
            ga_copy(tower, o).wait_send()

        @pl.loop(1, 16)
        def _(o):
            zc_copy(tower, o).wait_send()
            fd_copy(tower, o).wait_send()


def ring_k(ring, d, k, c):
    ring(d, k, c).wait_recv()
    ring(d, k + 1, c).start()


def local(hv, hc, wv, wc, match, multiplier, offset):
    vmem = pl.BlockSpec(memory_space=pltpu.VMEM)
    smem = pl.BlockSpec(memory_space=pltpu.SMEM)
    anywhere = pl.BlockSpec(memory_space=pl.ANY)
    dma = pltpu.SemaphoreType.DMA
    return pl.pallas_call(
        kernel,
        out_shape=(
            jax.ShapeDtypeStruct((TOK, D), BF16),
            jax.ShapeDtypeStruct((TOK, D), BF16),
            jax.ShapeDtypeStruct((32, E), F32),
            jax.ShapeDtypeStruct((32, E), F32),
        ),
        in_specs=[anywhere] * 4 + [vmem, smem, smem],
        out_specs=(vmem,) * 4,
        scratch_shapes=[
            pltpu.VMEM((2, D, E), BF16),
            pltpu.VMEM((2, 8, TOK, D), BF16),
            pltpu.VMEM((2, D, 8 * TOK), BF16),
            pltpu.VMEM((2, TOK, E), F32),
            pltpu.VMEM((2, TOK, 1), F32),
            pltpu.VMEM((9, 2 * TOK, E), BF16),
            pltpu.VMEM((2 * TOK, E), BF16),
            pltpu.VMEM((9, 2 * TOK, E), F32),
            pltpu.VMEM((2 * TOK, E), F32),
            pltpu.VMEM((2, 8, TOK, E), BF16),
            pltpu.VMEM((2, 8, TOK, E), BF16),
            pltpu.VMEM((TOK, E), BF16),
            pltpu.VMEM((TOK, E), BF16),
            pltpu.VMEM((2, 8, TOK, 128), BF16),
            pltpu.VMEM((2, 8, TOK, 128), BF16),
            pltpu.VMEM((2, 4, NZ, 16, 128), BF16),
            pltpu.VMEM((2, 4, NZ, 16, 128), BF16),
            pltpu.VMEM((2, NZ, 16, 128), BF16),
            pltpu.VMEM((2, NZ, 16, 128), BF16),
            pltpu.VMEM((2, 16, 16, 128), F32),
            dma((4,)),
            dma((2, 8, 2)),
            dma((2, 8, 2)),
            dma((2, 8, 2)),
            dma((2, 8, 2)),
            dma((2,)),
            dma((2,)),
            dma((2, 3)),
            dma((2, 3)),
            dma((2, 4)),
            dma((2, 4)),
            dma((2, 7)),
            dma((2, 7)),
            dma((2, 3)),
            dma((2, 3)),
            dma((2, 15)),
            dma((2, 15)),
            dma((2, 15)),
            dma((2, 15)),
        ],
        compiler_params=pltpu.CompilerParams(
            collective_id=0, has_side_effects=True, vmem_limit_bytes=60 << 20
        ),
    )(hv, hc, wv, wc, match.reshape(32, TOK), multiplier, offset)


def solution(mesh):
    placed = (P(("grp", "blk"), None), P(("grp", "blk"), None), P(), P(), P("grp"), P(), P())
    return jax.shard_map(
        local,
        mesh=mesh,
        in_specs=placed,
        out_specs=(
            P(("grp", "blk"), None),
            P(("grp", "blk"), None),
            P("blk", None),
            P("blk", None),
        ),
        check_vma=False,
    )
```

```python
import jax
import jax.numpy as jnp
from jax import lax
from jax.experimental import pallas as pl
from jax.experimental.pallas import tpu as pltpu
from jax.sharding import PartitionSpec as P

MESH = pl.DeviceIdType.MESH
F32 = jnp.float32
BF16 = jnp.bfloat16
NX, NZ, TOK, D, E = 4, 16, 128, 1024, 1024
NC = 4
ROWS = TOK // NC
LATE = ((0, 1), (2, 3))
AHEAD = ((2, 3), (0, 1))
CLIP, TEXT = 0, 1


def kernel(
    hv_hbm,
    hc_hbm,
    wv_hbm,
    wc_hbm,
    match_ref,
    scale_ref,
    shift_ref,
    clip_hid,
    text_hid,
    clip_wg,
    text_wg,
    w,
    hx,
    ht,
    unit,
    length,
    tt,
    emb,
    part,
    cacc,
    back_in,
    back_out,
    share_out,
    share_in,
    g_out,
    g_in,
    y_out,
    y_in,
    z_out,
    z_in,
    f_in,
    hid_out,
    wg_out,
    load_sem,
    out_sem,
    ring_s,
    ring_r,
    back_s,
    back_r,
    share_s,
    share_r,
    hid_s,
    hid_r,
    rel_s,
    rel_r,
    ga_s,
    ga_r,
    yb_s,
    yb_r,
    zc_s,
    zc_r,
    fd_s,
    fd_r,
):
    grp = lax.axis_index("grp")
    blk = lax.axis_index("blk")
    yh, x, core = grp // 8, (grp // 2) % 4, grp % 2
    yl, z = blk // NZ, blk % NZ
    y = yh * 2 + yl
    q = x * 2 + core

    def place(x=x, y=y, z=z, core=core):
        return ((y // 2) * 8 + x * 2 + core, (y % 2) * NZ + z)

    right, left = place(z=(z + 1) % NZ), place(z=(z + NZ - 1) % NZ)
    partner = place(y=yh * 2 + 1 - yl)
    sibling = place(core=1 - core)

    def remote(src, dst, s, r, device):
        return pltpu.make_async_remote_copy(
            src_ref=src, dst_ref=dst, send_sem=s, recv_sem=r, device_id=device, device_id_type=MESH
        )

    loads = [
        pltpu.make_async_copy(wc_hbm, w.at[TEXT], load_sem.at[0]),
        pltpu.make_async_copy(hc_hbm, hx.at[TEXT, q], load_sem.at[1]),
        pltpu.make_async_copy(wv_hbm, w.at[CLIP], load_sem.at[2]),
        pltpu.make_async_copy(hv_hbm, hx.at[CLIP, q], load_sem.at[3]),
    ]
    for copy in loads:
        copy.start()

    barrier = pltpu.get_barrier_semaphore()
    near = [right, left, sibling]
    near += [place(x=(x + o) % 4) for o in (1, 2, 3)] + [place(y=(y + o) % 4) for o in (1, 2, 3)]
    for device in near:
        pl.semaphore_signal(barrier, 1, device_id=device, device_id_type=MESH)

    def project(tower):
        raw = jnp.dot(hx[tower, q], w[tower], preferred_element_type=F32)
        size = jnp.sqrt(jnp.sum(raw * raw, axis=1, keepdims=True) + 1e-06)
        vec = raw / size
        unit[tower] = vec
        length[tower] = size
        return vec.astype(BF16)

    def ring(d, k, c):
        first = isinstance(k, int) and k == 1
        last = isinstance(k, int) and k == 8
        src = tt.at[k - 1, pl.ds((0 if first else TOK * d) + ROWS * c, ROWS)]
        dst = tt.at[k, pl.ds((0 if last else TOK * d) + ROWS * c, ROWS)]
        return remote(src, dst, ring_s.at[d, k - 1, c], ring_r.at[d, k - 1, c], (right, left)[d])

    def back(d, k, c):
        rows = pl.ds(ROWS * c, ROWS)
        return remote(
            back_out.at[d, k - 1, rows],
            back_in.at[d, k - 1, rows],
            back_s.at[d, k - 1, c],
            back_r.at[d, k - 1, c],
            (left, right)[d],
        )

    def hid_copy(tower, o, wait=False):
        index = ((x - o + 4) % 4) * 2 + core if wait else q
        return remote(
            hx.at[tower, index],
            hx.at[tower, index],
            hid_s.at[tower, o - 1],
            hid_r.at[tower, o - 1],
            place(x=(x + o) % NX),
        )

    def relay(tower, o, wait=False):
        index = ((x - o + 4) % 4) * 2 + ((1 - core) if wait else core)
        return remote(
            hx.at[tower, index], hx.at[tower, index], rel_s.at[tower, o], rel_r.at[tower, o], sibling
        )

    loads[0].wait()
    loads[1].wait()
    tt[0, pl.ds(0, TOK)] = project(TEXT)
    pl.semaphore_wait(barrier, len(near))
    for i in range(NC):
        for d in (0, 1):
            ring(d, 1, (LATE[d] + AHEAD[d])[i]).start()
    loads[2].wait()
    loads[3].wait()
    emb[pl.ds(0, TOK)] = project(CLIP)
    share_emb = remote(
        emb.at[pl.ds(0, TOK)], emb.at[pl.ds(TOK, TOK)], share_s.at[0], share_r.at[0], partner
    )
    share_emb.start()
    for tower in (CLIP, TEXT):
        for o in (1, 3, 2):
            hid_copy(tower, o).start()
        relay(tower, 0).start()

    scale = scale_ref[0]
    shift = shift_ref[0]

    def work(k, rows):
        base0 = (yl * NZ + (z - k + NZ) % NZ) * TOK
        base1 = (yl * NZ + (z + k) % NZ) * TOK
        t = tt[k, pl.ds(0, rows)]
        a = emb[...]
        scores = scale * lax.dot_general(
            t, a, (((1,), (1,)), ((), ())), preferred_element_type=F32
        ) + shift
        row = lax.broadcasted_iota(jnp.int32, (rows, 2 * TOK), 0)
        place_of = jnp.where(row < TOK, base0 + row, base1 + row - TOK)
        wanted = jnp.concatenate(
            [match_ref[pl.ds(blk, 1), :], match_ref[pl.ds((1 - yl) * NZ + z, 1), :]], axis=1
        )
        hit = place_of == wanted
        flipped = jnp.where(hit, scores, -scores)
        coef = (jnp.where(hit, -scale, scale) / (1.0 + jnp.exp(flipped))).astype(BF16)
        part[k, pl.ds(0, rows)] = jnp.dot(coef, a, preferred_element_type=F32)
        return lax.dot_general(coef, t, (((0,), (0,)), ((), ())), preferred_element_type=F32)

    def forward(k):
        for i in range(NC):
            for d in (0, 1):
                c = (LATE[d] + AHEAD[d])[i]
                ring(d, k, c).wait_recv()
                if not (isinstance(k, int) and k == 7 and c in AHEAD[d]):
                    ring(d, k + 1, c).start()

    forward(1)
    share_emb.wait_recv()
    cacc[...] = work(0, TOK)

    @pl.loop(2, 7)
    def _(k):
        forward(k)
        cacc[...] += work(k - 1, 2 * TOK)

    def run(d, k, c):
        return part[k, pl.ds((0 if k == 8 else TOK * d) + ROWS * c, ROWS)]

    def send_fresh(d, k, c):
        back_out[d, k - 1, pl.ds(ROWS * c, ROWS)] = run(d, k, c).astype(BF16)
        back(d, k, c).start()

    def send_sum(d, k, c):
        rows = pl.ds(ROWS * c, ROWS)
        back(d, k + 1, c).wait_recv()
        back_out[d, k - 1, rows] = (run(d, k, c) + back_in[d, k, rows].astype(F32)).astype(BF16)
        back(d, k, c).start()

    forward(7)

    @pl.loop(6, 8)
    def _(k):
        cacc[...] += work(k, 2 * TOK)

    for i in (0, 1):
        for d in (0, 1):
            send_fresh(d, 7, AHEAD[d][i])
    for i in (0, 1):
        for d in (0, 1):
            ring(d, 8, LATE[d][i]).wait_recv()
    cacc[...] += work(8, TOK)
    for i in (0, 1):
        for d in (0, 1):
            send_fresh(d, 8, LATE[d][i])

    share_out[...] = cacc[pl.ds(TOK, TOK)].astype(BF16)
    share_grad = remote(share_out, share_in, share_s.at[1], share_r.at[1], partner)
    share_grad.start()

    def ga_copy(tower, o, wait=False):
        to = (q + o) % 8
        return remote(
            g_out.at[tower, to],
            g_in.at[tower, (q - o + 8) % 8 if wait else q],
            ga_s.at[tower, o - 1],
            ga_r.at[tower, o - 1],
            place(x=to // 2, core=to % 2),
        )

    def yb_copy(tower, o):
        to = (y + o) % 4
        return remote(
            y_out.at[tower, to],
            y_in.at[tower, o],
            yb_s.at[tower, o - 1],
            yb_r.at[tower, o - 1],
            place(y=to),
        )

    def zc_copy(tower, o):
        to = (z + o) % NZ
        return remote(
            z_out.at[tower, to], z_in.at[tower, o], zc_s.at[tower], zc_r.at[tower], place(z=to)
        )

    def zc_all(tower):
        rest = pl.ds(1, NZ - 1)
        return remote(
            z_out.at[tower, rest], z_in.at[tower, rest], zc_s.at[tower], zc_r.at[tower], right
        )

    def fd_copy(tower, o):
        return remote(
            f_in.at[tower, 0],
            f_in.at[tower, o],
            fd_s.at[tower],
            fd_r.at[tower],
            ((grp + o) % 16, blk),
        )

    def fd_all(tower):
        rest = pl.ds(1, 15)
        return remote(
            f_in.at[tower, rest], f_in.at[tower, rest], fd_s.at[tower], fd_r.at[tower], right
        )

    def raw_grad(tower, grad):
        vec = unit[tower]
        radial = jnp.sum(vec * grad, axis=1, keepdims=True)
        raw = ((grad - vec * radial) / length[tower]).astype(BF16)
        for j in range(8):
            g_out[tower, j] = raw[:, 128 * j : 128 * (j + 1)]

        @pl.loop(1, 8)
        def _(o):
            ga_copy(tower, o).start()

    def hidden_copy(tower):
        return pltpu.make_async_copy(
            hid_out.at[tower], (clip_hid, text_hid)[tower], out_sem.at[tower]
        )

    def hidden_grad(tower):
        raw = jnp.concatenate([g_out[tower, j] for j in range(8)], axis=1)
        hid_out[tower] = lax.dot_general(
            raw, w[tower], (((1,), (1,)), ((), ())), preferred_element_type=F32
        ).astype(BF16)
        hidden_copy(tower).start()

    def turn(tower, *blocks):
        for j in blocks:
            ht[tower, :, pl.ds(128 * j, 128)] = hx[tower, j].T

    def gathered(tower):
        g_in[tower, q] = g_out[tower, q]

        @pl.loop(1, 8)
        def _(o):
            ga_copy(tower, o, True).wait_recv()

    def weight(tower, own):
        to = yl if own else 1 - yl
        g = g_in[tower].reshape(8 * TOK, 128)
        rows = pl.ds(pl.multiple_of(512 * to, 512), 512)
        term = jnp.dot(ht[tower, rows, :], g, preferred_element_type=F32)
        term = term.reshape(NZ, 2, 16, 128).astype(BF16)
        for yh_to in (0, 1):
            y_out[tower, yh_to * 2 + to] = term[:, yh_to]
        for o in (2,) if own else (1, 3):
            yb_copy(tower, o).start()

    def over_y(tower):
        total = y_out[tower, y].astype(F32)
        for o in (1, 3, 2):
            yb_copy(tower, o).wait_recv()
            total = total + y_in[tower, o].astype(F32)
        z_out[tower] = total.astype(BF16)

    def send_z(tower):
        for o in (8, 7, 9, 6, 10, 5, 11, 4, 12, 3, 13, 2, 14, 1, 15):
            zc_copy(tower, o).start()

    def over_z(tower):
        z_in[tower, 0] = z_out[tower, z]
        zc_all(tower).wait_recv()
        f_in[tower, 0] = jnp.sum(z_in[tower].astype(F32), axis=0).astype(BF16)
        for o in range(1, 16):
            fd_copy(tower, o).start()

    def weight_copy(tower):
        return pltpu.make_async_copy(
            wg_out.at[tower], (clip_wg, text_wg)[tower], out_sem.at[2 + tower]
        )

    def finish(tower):
        fd_all(tower).wait_recv()
        for j in range(16):
            piece = f_in[tower, (grp - j + 16) % 16].astype(F32)
            wg_out[tower, pl.ds(16 * (j // 8), 16), pl.ds(128 * (j % 8), 128)] = piece
        weight_copy(tower).start()

    def relays(tower):
        for o in (1, 2, 3):
            hid_copy(tower, o, True).wait_recv()
            relay(tower, o).start()

    def relays_done(tower):
        for o in range(4):
            relay(tower, o, True).wait_recv()

    def clip_raw():
        share_grad.wait_recv()
        raw_grad(CLIP, cacc[pl.ds(0, TOK)] + share_in[...].astype(F32))

    def ring_left(k):
        for d in (0, 1):
            for c in range(NC) if k < 8 else LATE[d]:
                ring(d, k, c).wait_send()

    def hidden_left():
        for tower in (CLIP, TEXT):
            for o in range(4):
                relay(tower, o).wait_send()
            for o in (1, 2, 3):
                hid_copy(tower, o).wait_send()

    def columns_left(tower):
        @pl.loop(1, 8)
        def _(o):
            ga_copy(tower, o).wait_send()

    def sums_left(tower):
        for o in (1, 2, 3):
            yb_copy(tower, o).wait_send()

    pieces = {
        0: lambda: relays(CLIP),
        2: lambda: ring_left(1),
        3: lambda: relays_done(CLIP),
        4: lambda: turn(CLIP, 0, 1),
        5: lambda: turn(CLIP, 2, 3),
        6: lambda: clip_raw(),
        7: lambda: hidden_grad(CLIP),
        8: lambda: turn(CLIP, 4, 5),
        9: lambda: turn(CLIP, 6, 7),
        10: lambda: relays(TEXT),
        11: lambda: gathered(CLIP),
        12: lambda: weight(CLIP, False),
        13: lambda: weight(CLIP, True),
        14: lambda: relays_done(TEXT),
        15: lambda: turn(TEXT, 0, 1),
        16: lambda: turn(TEXT, 2, 3),
        17: lambda: turn(TEXT, 4, 5),
        18: lambda: turn(TEXT, 6, 7),
        19: lambda: over_y(CLIP),
        20: lambda: ring_left(2),
        21: lambda: ring_left(3),
        22: lambda: ring_left(4),
        23: lambda: ring_left(5),
        24: lambda: ring_left(6),
        25: lambda: ring_left(7),
        26: lambda: ring_left(8),
    }
    for j in range(6, -1, -1):
        for i in range(4):
            for d in (0, 1):
                if i >= 2:
                    send_sum(d, j + 1, LATE[d][i - 2])
                elif j >= 1:
                    send_sum(d, j, AHEAD[d][i])
                else:
                    back(d, 1, AHEAD[d][i]).wait_recv()
            pieces.get((6 - j) * 4 + i, lambda: None)()
    for i in (0, 1):
        for d in (0, 1):
            back(d, 1, LATE[d][i]).wait_recv()

    grad = part[0, pl.ds(0, TOK)] + back_in[0, 0].astype(F32) + back_in[1, 0].astype(F32)
    raw_grad(TEXT, grad)
    send_z(CLIP)
    hidden_grad(TEXT)
    gathered(TEXT)
    weight(TEXT, False)
    weight(TEXT, True)
    over_z(CLIP)
    over_y(TEXT)
    send_z(TEXT)
    for d in (0, 1):
        for c in range(NC):

            @pl.loop(1, 8)
            def _(k):
                back(d, k, c).wait_send()

        for c in LATE[d]:
            back(d, 8, c).wait_send()
    finish(CLIP)
    hidden_left()
    over_z(TEXT)
    share_emb.wait_send()
    share_grad.wait_send()
    for tower in (CLIP, TEXT):
        columns_left(tower)
        sums_left(tower)
        zc_all(tower).wait_send()
    fd_all(CLIP).wait_send()
    hidden_copy(CLIP).wait()
    hidden_copy(TEXT).wait()
    weight_copy(CLIP).wait()
    finish(TEXT)
    fd_all(TEXT).wait_send()
    weight_copy(TEXT).wait()


def hand_over(*refs):
    for i in range(4):
        refs[4 + i][...] = refs[i][...]


def local(hv, hc, wv, wc, match, multiplier, offset):
    vmem = pl.BlockSpec(memory_space=pltpu.VMEM)
    smem = pl.BlockSpec(memory_space=pltpu.SMEM)
    anywhere = pl.BlockSpec(memory_space=pl.ANY)
    dma = pltpu.SemaphoreType.DMA
    shapes = (
        jax.ShapeDtypeStruct((TOK, D), BF16),
        jax.ShapeDtypeStruct((TOK, D), BF16),
        jax.ShapeDtypeStruct((32, E), F32),
        jax.ShapeDtypeStruct((32, E), F32),
    )
    results = pl.pallas_call(
        kernel,
        out_shape=shapes,
        in_specs=[anywhere] * 4 + [vmem, smem, smem],
        out_specs=(anywhere,) * 4,
        scratch_shapes=[
            pltpu.VMEM((2, D, E), BF16),
            pltpu.VMEM((2, 8, TOK, D), BF16),
            pltpu.VMEM((2, D, 8 * TOK), BF16),
            pltpu.VMEM((2, TOK, E), F32),
            pltpu.VMEM((2, TOK, 1), F32),
            pltpu.VMEM((9, 2 * TOK, E), BF16),
            pltpu.VMEM((2 * TOK, E), BF16),
            pltpu.VMEM((9, 2 * TOK, E), F32),
            pltpu.VMEM((2 * TOK, E), F32),
            pltpu.VMEM((2, 8, TOK, E), BF16),
            pltpu.VMEM((2, 8, TOK, E), BF16),
            pltpu.VMEM((TOK, E), BF16),
            pltpu.VMEM((TOK, E), BF16),
            pltpu.VMEM((2, 8, TOK, 128), BF16),
            pltpu.VMEM((2, 8, TOK, 128), BF16),
            pltpu.VMEM((2, 4, NZ, 16, 128), BF16),
            pltpu.VMEM((2, 4, NZ, 16, 128), BF16),
            pltpu.VMEM((2, NZ, 16, 128), BF16),
            pltpu.VMEM((2, NZ, 16, 128), BF16),
            pltpu.VMEM((2, 16, 16, 128), BF16),
            pltpu.VMEM((2, TOK, D), BF16),
            pltpu.VMEM((2, 32, E), F32),
            dma((4,)),
            dma((4,)),
            dma((2, 8, NC)),
            dma((2, 8, NC)),
            dma((2, 8, NC)),
            dma((2, 8, NC)),
            dma((2,)),
            dma((2,)),
            dma((2, 3)),
            dma((2, 3)),
            dma((2, 4)),
            dma((2, 4)),
            dma((2, 7)),
            dma((2, 7)),
            dma((2, 3)),
            dma((2, 3)),
            dma((2,)),
            dma((2,)),
            dma((2,)),
            dma((2,)),
        ],
        compiler_params=pltpu.CompilerParams(
            collective_id=0, has_side_effects=True, vmem_limit_bytes=60 << 20
        ),
    )(hv, hc, wv, wc, match.reshape(32, TOK), multiplier, offset)
    return pl.pallas_call(
        hand_over,
        out_shape=shapes,
        in_specs=[vmem] * 4,
        out_specs=(vmem,) * 4,
    )(*results)


def solution(mesh):
    placed = (P(("grp", "blk"), None), P(("grp", "blk"), None), P(), P(), P("grp"), P(), P())
    return jax.shard_map(
        local,
        mesh=mesh,
        in_specs=placed,
        out_specs=(
            P(("grp", "blk"), None),
            P(("grp", "blk"), None),
            P("blk", None),
            P("blk", None),
        ),
        check_vma=False,
    )
```

```python
import jax
import jax.numpy as jnp
from jax import lax
from jax.experimental import pallas as pl
from jax.experimental.pallas import tpu as pltpu
from jax.sharding import PartitionSpec as P

MESH = pl.DeviceIdType.MESH
F32 = jnp.float32
BF16 = jnp.bfloat16
NX, NZ, TOK, D, E = 4, 16, 128, 1024, 1024
NC = 4
ROWS = TOK // NC
HALF = TOK // 2
LATE = ((0, 2), (1, 3))
AHEAD = ((1, 3), (0, 2))
COLUMNS = ((2, 1), (2, 0), (1, 1), (3, 1), (1, 0), (3, 0), (0, 1))
ALL_GRP = tuple((1,) + p for p in COLUMNS) + ((1, 0, 0),) + tuple((0,) + p for p in COLUMNS)
CLIP, TEXT = 0, 1


def kernel(
    hv_hbm,
    hc_hbm,
    wv_hbm,
    wc_hbm,
    match_ref,
    scale_ref,
    shift_ref,
    clip_hid,
    text_hid,
    f_all,
    w,
    hx,
    ht,
    unit,
    length,
    tt,
    emb,
    part,
    cacc,
    back_in,
    back_out,
    share_out,
    share_in,
    raw_out,
    g_out,
    g_in,
    w_first,
    y_out,
    y_in,
    z_out,
    z_in,
    f_own,
    hid_out,
    load_sem,
    out_sem,
    ring_s,
    ring_r,
    back_s,
    back_r,
    share_s,
    share_r,
    hid_s,
    hid_r,
    rel_s,
    rel_r,
    ga_s,
    ga_r,
    yb_s,
    yb_r,
    zc_s,
    zc_r,
    fd_s,
    fd_r,
):
    grp = lax.axis_index("grp")
    blk = lax.axis_index("blk")
    yh, x, core = grp // 8, (grp // 2) % 4, grp % 2
    yl, z = blk // NZ, blk % NZ
    y = yh * 2 + yl
    q = x * 2 + core

    def place(x=x, y=y, z=z, core=core):
        return ((y // 2) * 8 + x * 2 + core, (y % 2) * NZ + z)

    right, left = place(z=(z + 1) % NZ), place(z=(z + NZ - 1) % NZ)
    partner = place(y=yh * 2 + 1 - yl)
    sibling = place(core=1 - core)

    def remote(src, dst, s, r, device):
        return pltpu.make_async_remote_copy(
            src_ref=src, dst_ref=dst, send_sem=s, recv_sem=r, device_id=device, device_id_type=MESH
        )

    loads = [
        pltpu.make_async_copy(wc_hbm, w.at[TEXT], load_sem.at[0]),
        pltpu.make_async_copy(hc_hbm, hx.at[TEXT, q], load_sem.at[1]),
        pltpu.make_async_copy(wv_hbm, w.at[CLIP], load_sem.at[2]),
        pltpu.make_async_copy(hv_hbm, hx.at[CLIP, q], load_sem.at[3]),
    ]
    for copy in loads:
        copy.start()

    barrier = pltpu.get_barrier_semaphore()
    near = [right, left, sibling]
    near += [place(x=(x + o) % 4) for o in (1, 2, 3)] + [place(y=(y + o) % 4) for o in (1, 2, 3)]
    for device in near:
        pl.semaphore_signal(barrier, 1, device_id=device, device_id_type=MESH)

    def project(tower):
        raw = jnp.dot(hx[tower, q], w[tower], preferred_element_type=F32)
        size = jnp.sqrt(jnp.sum(raw * raw, axis=1, keepdims=True) + 1e-06)
        vec = raw / size
        unit[tower] = vec
        length[tower] = size
        return vec.astype(BF16)

    def ring(d, k, c):
        first = isinstance(k, int) and k == 1
        last = isinstance(k, int) and k == 8
        src = tt.at[k - 1, pl.ds((0 if first else TOK * d) + ROWS * c, ROWS)]
        dst = tt.at[k, pl.ds((0 if last else TOK * d) + ROWS * c, ROWS)]
        return remote(src, dst, ring_s.at[d, k - 1, c], ring_r.at[d, k - 1, c], (right, left)[d])

    def back(d, k, c):
        rows = pl.ds(ROWS * c, ROWS)
        return remote(
            back_out.at[d, k - 1, rows],
            back_in.at[d, k - 1, rows],
            back_s.at[d, k - 1, c],
            back_r.at[d, k - 1, c],
            (left, right)[d],
        )

    def hid_copy(tower, o, wait=False):
        index = ((x - o + 4) % 4) * 2 + core if wait else q
        return remote(
            hx.at[tower, index],
            hx.at[tower, index],
            hid_s.at[tower, o - 1],
            hid_r.at[tower, o - 1],
            place(x=(x + o) % NX),
        )

    def relay(tower, o, wait=False):
        index = ((x - o + 4) % 4) * 2 + ((1 - core) if wait else core)
        return remote(
            hx.at[tower, index], hx.at[tower, index], rel_s.at[tower, o], rel_r.at[tower, o], sibling
        )

    loads[0].wait()
    loads[1].wait()
    tt[0, pl.ds(0, TOK)] = project(TEXT)
    pl.semaphore_wait(barrier, len(near))
    for i in range(NC):
        for d in (0, 1):
            ring(d, 1, (LATE[d] + AHEAD[d])[i]).start()
    loads[2].wait()
    loads[3].wait()
    emb[pl.ds(0, TOK)] = project(CLIP)
    share_emb = remote(
        emb.at[pl.ds(0, TOK)], emb.at[pl.ds(TOK, TOK)], share_s.at[0], share_r.at[0], partner
    )
    share_emb.start()
    for tower in (CLIP, TEXT):
        for o in (1, 3, 2):
            hid_copy(tower, o).start()
        relay(tower, 0).start()

    scale = scale_ref[0]
    shift = shift_ref[0]

    def work(k, rows):
        base0 = (yl * NZ + (z - k + NZ) % NZ) * TOK
        base1 = (yl * NZ + (z + k) % NZ) * TOK
        t = tt[k, pl.ds(0, rows)]
        a = emb[...]
        scores = scale * lax.dot_general(
            t, a, (((1,), (1,)), ((), ())), preferred_element_type=F32
        ) + shift
        row = lax.broadcasted_iota(jnp.int32, (rows, 2 * TOK), 0)
        place_of = jnp.where(row < TOK, base0 + row, base1 + row - TOK)
        wanted = jnp.concatenate(
            [match_ref[pl.ds(blk, 1), :], match_ref[pl.ds((1 - yl) * NZ + z, 1), :]], axis=1
        )
        hit = place_of == wanted
        flipped = jnp.where(hit, scores, -scores)
        coef = (jnp.where(hit, -scale, scale) / (1.0 + jnp.exp(flipped))).astype(BF16)
        part[k, pl.ds(0, rows)] = jnp.dot(coef, a, preferred_element_type=F32)
        return lax.dot_general(coef, t, (((0,), (0,)), ((), ())), preferred_element_type=F32)

    def forward(k):
        for i in range(NC):
            for d in (0, 1):
                c = (LATE[d] + AHEAD[d])[i]
                ring(d, k, c).wait_recv()
                if not (isinstance(k, int) and k == 7 and c in AHEAD[d]):
                    ring(d, k + 1, c).start()

    forward(1)
    share_emb.wait_recv()
    cacc[...] = work(0, TOK)

    @pl.loop(2, 7)
    def _(k):
        forward(k)
        cacc[...] += work(k - 1, 2 * TOK)

    def run(d, k, c):
        return part[k, pl.ds((0 if k == 8 else TOK * d) + ROWS * c, ROWS)]

    def send_fresh(d, k, c):
        back_out[d, k - 1, pl.ds(ROWS * c, ROWS)] = run(d, k, c).astype(BF16)
        back(d, k, c).start()

    def send_sum(d, k, c):
        rows = pl.ds(ROWS * c, ROWS)
        back(d, k + 1, c).wait_recv()
        back_out[d, k - 1, rows] = (run(d, k, c) + back_in[d, k, rows].astype(F32)).astype(BF16)
        back(d, k, c).start()

    forward(7)

    @pl.loop(6, 8)
    def _(k):
        cacc[...] += work(k, 2 * TOK)

    for i in (0, 1):
        for d in (0, 1):
            send_fresh(d, 7, AHEAD[d][i])
    for i in (0, 1):
        for d in (0, 1):
            ring(d, 8, LATE[d][i]).wait_recv()
    cacc[...] += work(8, TOK)
    for i in (0, 1):
        for d in (0, 1):
            send_fresh(d, 8, LATE[d][i])

    share_out[...] = cacc[pl.ds(TOK, TOK)].astype(BF16)
    share_grad = remote(share_out, share_in, share_s.at[1], share_r.at[1], partner)
    share_grad.start()

    def ga_copy(tower, h, dx, dc, wait=False):
        to = ((x + dx) % 4) * 2 + (core + dc) % 2
        come = ((x - dx + 4) % 4) * 2 + (core + dc) % 2
        return remote(
            g_out.at[tower, h, to],
            g_in.at[tower, h, come if wait else q],
            ga_s.at[tower, h, dx * 2 + dc - 1],
            ga_r.at[tower, h, dx * 2 + dc - 1],
            place(x=(x + dx) % 4, core=(core + dc) % 2),
        )

    def yb_copy(tower, o):
        to = (y + o) % 4
        return remote(
            y_out.at[tower, to],
            y_in.at[tower, o],
            yb_s.at[tower, o - 1],
            yb_r.at[tower, o - 1],
            place(y=to),
        )

    def zc_copy(tower, o):
        to = (z + o) % NZ
        return remote(
            z_out.at[tower, to], z_in.at[tower, o], zc_s.at[tower], zc_r.at[tower], place(z=to)
        )

    def zc_all(tower):
        rest = pl.ds(1, NZ - 1)
        return remote(
            z_out.at[tower, rest], z_in.at[tower, rest], zc_s.at[tower], zc_r.at[tower], right
        )

    def fd_copy(tower, dy, dx, dc):
        to = ((yh + dy) % 2) * 8 + ((x + dx) % 4) * 2 + (core + dc) % 2
        return remote(
            f_own.at[tower], f_all.at[tower, grp], fd_s.at[tower], fd_r.at[tower], (to, blk)
        )

    def fd_all(tower):
        rest = f_all.at[tower, pl.ds(0, 15)]
        return remote(rest, rest, fd_s.at[tower], fd_r.at[tower], right)

    def raw_grad(tower, h, grad):
        rows = pl.ds(HALF * h, HALF)
        vec = unit[tower, rows]
        radial = jnp.sum(vec * grad, axis=1, keepdims=True)
        raw = ((grad - vec * radial) / length[tower, rows]).astype(BF16)
        for j in range(8):
            g_out[tower, h, j] = raw[:, 128 * j : 128 * (j + 1)]
        for dx, dc in COLUMNS:
            ga_copy(tower, h, dx, dc).start()
        raw_out[tower, rows] = raw

    def hidden_copy(tower):
        return pltpu.make_async_copy(
            hid_out.at[tower], (clip_hid, text_hid)[tower], out_sem.at[tower]
        )

    def hidden_grad(tower):
        hid_out[tower] = lax.dot_general(
            raw_out[tower], w[tower], (((1,), (1,)), ((), ())), preferred_element_type=F32
        ).astype(BF16)
        hidden_copy(tower).start()

    def turn(tower, h, *pairs):
        rows = pl.ds(HALF * h, HALF)
        for j in pairs:
            two = jnp.concatenate([hx[tower, 2 * j, rows], hx[tower, 2 * j + 1, rows]], axis=0)
            ht[tower, :, pl.ds(512 * h + 128 * j, 128)] = two.T

    def gathered(tower, h):
        g_in[tower, h, q] = g_out[tower, h, q]
        for dx, dc in COLUMNS[::-1]:
            ga_copy(tower, h, dx, dc, True).wait_recv()

    def product(tower, h, rows):
        g = g_in[tower, h].reshape(8 * HALF, 128)
        return jnp.dot(ht[tower, rows, pl.ds(512 * h, 512)], g, preferred_element_type=F32)

    def weight_first(tower):
        gathered(tower, 0)
        w_first[...] = product(tower, 0, pl.ds(0, D))

    def weight(tower, own):
        to = yl if own else 1 - yl
        rows = pl.ds(pl.multiple_of(512 * to, 512), 512)
        term = w_first[rows] + product(tower, 1, rows)
        term = term.reshape(NZ, 2, 16, 128).astype(BF16)
        for yh_to in (0, 1):
            y_out[tower, yh_to * 2 + to] = term[:, yh_to]
        for o in (2,) if own else (1, 3):
            yb_copy(tower, o).start()

    def over_y(tower):
        total = y_out[tower, y].astype(F32)
        for o in (1, 3, 2):
            yb_copy(tower, o).wait_recv()
            total = total + y_in[tower, o].astype(F32)
        z_out[tower] = total.astype(BF16)

    def send_z(tower):
        for o in (8, 7, 9, 6, 10, 5, 11, 4, 12, 3, 13, 2, 14, 1, 15):
            zc_copy(tower, o).start()

    def own_copy(tower):
        return pltpu.make_async_copy(f_own.at[tower], f_all.at[tower, grp], out_sem.at[2 + tower])

    def over_z(tower):
        z_in[tower, 0] = z_out[tower, z]
        zc_all(tower).wait_recv()
        f_own[tower] = jnp.sum(z_in[tower].astype(F32), axis=0).astype(BF16)
        for dy, dx, dc in ALL_GRP:
            fd_copy(tower, dy, dx, dc).start()
        own_copy(tower).start()

    def relays(tower):
        for o in (1, 2, 3):
            hid_copy(tower, o, True).wait_recv()
            relay(tower, o).start()

    def relays_done(tower):
        for o in range(4):
            relay(tower, o, True).wait_recv()

    def clip_raw(h):
        if h == 0:
            share_grad.wait_recv()
        rows = pl.ds(HALF * h, HALF)
        raw_grad(CLIP, h, cacc[rows] + share_in[rows].astype(F32))

    def text_raw(h):
        rows = pl.ds(HALF * h, HALF)
        sums = back_in[0, 0, rows].astype(F32) + back_in[1, 0, rows].astype(F32)
        raw_grad(TEXT, h, part[0, rows] + sums)

    def ring_left(k):
        for d in (0, 1):
            for c in range(NC) if k < 8 else LATE[d]:
                ring(d, k, c).wait_send()

    def hidden_left():
        for tower in (CLIP, TEXT):
            for o in range(4):
                relay(tower, o).wait_send()
            for o in (1, 2, 3):
                hid_copy(tower, o).wait_send()

    def columns_left(tower):
        for h in (0, 1):
            for dx, dc in COLUMNS:
                ga_copy(tower, h, dx, dc).wait_send()

    def sums_left(tower):
        for o in (1, 2, 3):
            yb_copy(tower, o).wait_send()

    pieces = {
        0: lambda: relays(CLIP),
        2: lambda: ring_left(1),
        3: lambda: relays_done(CLIP),
        4: lambda: turn(CLIP, 0, 0, 1),
        5: lambda: turn(CLIP, 0, 2, 3),
        6: lambda: clip_raw(0),
        7: lambda: clip_raw(1),
        8: lambda: hidden_grad(CLIP),
        9: lambda: turn(CLIP, 1, 0, 1),
        10: lambda: turn(CLIP, 1, 2, 3),
        11: lambda: weight_first(CLIP),
        12: lambda: gathered(CLIP, 1),
        13: lambda: weight(CLIP, True),
        14: lambda: weight(CLIP, False),
        15: lambda: relays(TEXT),
        16: lambda: ring_left(2),
        17: lambda: relays_done(TEXT),
        18: lambda: turn(TEXT, 0, 0, 1),
        19: lambda: turn(TEXT, 0, 2, 3),
        20: lambda: turn(TEXT, 1, 0, 1),
        21: lambda: turn(TEXT, 1, 2, 3),
        22: lambda: over_y(CLIP),
        23: lambda: (ring_left(3), ring_left(4)),
        24: lambda: ring_left(5),
        25: lambda: (ring_left(6), ring_left(7)),
        26: lambda: ring_left(8),
    }
    for j in range(6, -1, -1):
        for i in range(4):
            for d in (0, 1):
                if i >= 2:
                    send_sum(d, j + 1, LATE[d][i - 2])
                elif j >= 1:
                    send_sum(d, j, AHEAD[d][i])
                else:
                    back(d, 1, AHEAD[d][i]).wait_recv()
            pieces.get((6 - j) * 4 + i, lambda: None)()
    for i in (0, 1):
        for d in (0, 1):
            back(d, 1, LATE[d][i]).wait_recv()
        text_raw(i)
    send_z(CLIP)
    hidden_grad(TEXT)
    weight_first(TEXT)
    gathered(TEXT, 1)
    weight(TEXT, True)
    weight(TEXT, False)
    over_z(CLIP)
    over_y(TEXT)
    send_z(TEXT)
    for d in (0, 1):
        for c in range(NC):

            @pl.loop(1, 8)
            def _(k):
                back(d, k, c).wait_send()

        for c in LATE[d]:
            back(d, 8, c).wait_send()
    fd_all(CLIP).wait()
    own_copy(CLIP).wait()
    hidden_left()
    share_emb.wait_send()
    share_grad.wait_send()
    columns_left(CLIP)
    sums_left(CLIP)
    zc_all(CLIP).wait_send()
    over_z(TEXT)
    columns_left(TEXT)
    sums_left(TEXT)
    zc_all(TEXT).wait_send()
    hidden_copy(CLIP).wait()
    hidden_copy(TEXT).wait()
    own_copy(TEXT).wait()
    fd_all(TEXT).wait()


def hand_over(clip_in, text_in, pieces, clip_hid, text_hid, clip_wg, text_wg):
    clip_hid[...] = clip_in[...]
    text_hid[...] = text_in[...]
    for tower, out in ((CLIP, clip_wg), (TEXT, text_wg)):
        for j in range(16):
            out[pl.ds(16 * (j // 8), 16), pl.ds(128 * (j % 8), 128)] = pieces[tower, j].astype(F32)


def local(hv, hc, wv, wc, match, multiplier, offset):
    vmem = pl.BlockSpec(memory_space=pltpu.VMEM)
    smem = pl.BlockSpec(memory_space=pltpu.SMEM)
    anywhere = pl.BlockSpec(memory_space=pl.ANY)
    dma = pltpu.SemaphoreType.DMA
    hidden = jax.ShapeDtypeStruct((TOK, D), BF16)
    gradient = jax.ShapeDtypeStruct((32, E), F32)
    results = pl.pallas_call(
        kernel,
        out_shape=(hidden, hidden, jax.ShapeDtypeStruct((2, 16, 16, 128), BF16)),
        in_specs=[anywhere] * 4 + [vmem, smem, smem],
        out_specs=(anywhere,) * 3,
        scratch_shapes=[
            pltpu.VMEM((2, D, E), BF16),
            pltpu.VMEM((2, 8, TOK, D), BF16),
            pltpu.VMEM((2, D, 8 * TOK), BF16),
            pltpu.VMEM((2, TOK, E), F32),
            pltpu.VMEM((2, TOK, 1), F32),
            pltpu.VMEM((9, 2 * TOK, E), BF16),
            pltpu.VMEM((2 * TOK, E), BF16),
            pltpu.VMEM((9, 2 * TOK, E), F32),
            pltpu.VMEM((2 * TOK, E), F32),
            pltpu.VMEM((2, 8, TOK, E), BF16),
            pltpu.VMEM((2, 8, TOK, E), BF16),
            pltpu.VMEM((TOK, E), BF16),
            pltpu.VMEM((TOK, E), BF16),
            pltpu.VMEM((2, TOK, E), BF16),
            pltpu.VMEM((2, 2, 8, HALF, 128), BF16),
            pltpu.VMEM((2, 2, 8, HALF, 128), BF16),
            pltpu.VMEM((D, 128), F32),
            pltpu.VMEM((2, 4, NZ, 16, 128), BF16),
            pltpu.VMEM((2, 4, NZ, 16, 128), BF16),
            pltpu.VMEM((2, NZ, 16, 128), BF16),
            pltpu.VMEM((2, NZ, 16, 128), BF16),
            pltpu.VMEM((2, 16, 128), BF16),
            pltpu.VMEM((2, TOK, D), BF16),
            dma((4,)),
            dma((4,)),
            dma((2, 8, NC)),
            dma((2, 8, NC)),
            dma((2, 8, NC)),
            dma((2, 8, NC)),
            dma((2,)),
            dma((2,)),
            dma((2, 3)),
            dma((2, 3)),
            dma((2, 4)),
            dma((2, 4)),
            dma((2, 2, 7)),
            dma((2, 2, 7)),
            dma((2, 3)),
            dma((2, 3)),
            dma((2,)),
            dma((2,)),
            dma((2,)),
            dma((2,)),
        ],
        compiler_params=pltpu.CompilerParams(
            collective_id=0, has_side_effects=True, vmem_limit_bytes=60 << 20
        ),
    )(hv, hc, wv, wc, match.reshape(32, TOK), multiplier, offset)
    return pl.pallas_call(
        hand_over,
        out_shape=(hidden, hidden, gradient, gradient),
        in_specs=[vmem] * 3,
        out_specs=(vmem,) * 4,
    )(*results)


def solution(mesh):
    placed = (P(("grp", "blk"), None), P(("grp", "blk"), None), P(), P(), P("grp"), P(), P())
    return jax.shard_map(
        local,
        mesh=mesh,
        in_specs=placed,
        out_specs=(
            P(("grp", "blk"), None),
            P(("grp", "blk"), None),
            P("blk", None),
            P("blk", None),
        ),
        check_vma=False,
    )
```

```python
import jax
import jax.numpy as jnp
from jax import lax
from jax.experimental import pallas as pl
from jax.experimental.pallas import tpu as pltpu
from jax.sharding import PartitionSpec as P

MESH = pl.DeviceIdType.MESH
F32 = jnp.float32
BF16 = jnp.bfloat16
NX, NZ, TOK, D, E = 4, 16, 128, 1024, 1024
NC = 4
ROWS = TOK // NC
HALF = TOK // 2
LATE = ((0, 2), (1, 3))
AHEAD = ((1, 3), (0, 2))
COLUMNS = ((2, 1), (2, 0), (1, 1), (3, 1), (1, 0), (3, 0), (0, 1))
ALL_GRP = tuple((1,) + p for p in COLUMNS) + ((1, 0, 0),) + tuple((0,) + p for p in COLUMNS)
CLIP, TEXT = 0, 1


def kernel(
    hv_hbm,
    hc_hbm,
    wv_hbm,
    wc_hbm,
    match_hbm,
    scale_hbm,
    shift_hbm,
    clip_hid,
    text_hid,
    f_all,
    w,
    hx,
    ht,
    unit,
    inverse,
    tt,
    emb,
    part,
    cacc,
    back_in,
    back_out,
    share_out,
    share_in,
    raw_out,
    g_out,
    g_in,
    w_first,
    y_out,
    y_in,
    z_out,
    z_in,
    match_ref,
    scale_ref,
    shift_ref,
    load_sem,
    ring_s,
    ring_r,
    back_s,
    back_r,
    share_s,
    share_r,
    hid_s,
    hid_r,
    rel_s,
    rel_r,
    ga_s,
    ga_r,
    yb_s,
    yb_r,
    zc_s,
    zc_r,
    fd_s,
    fd_r,
):
    grp = lax.axis_index("grp")
    blk = lax.axis_index("blk")
    yh, x, core = grp // 8, (grp // 2) % 4, grp % 2
    yl, z = blk // NZ, blk % NZ
    y = yh * 2 + yl
    q = x * 2 + core

    def place(x=x, y=y, z=z, core=core):
        return ((y // 2) * 8 + x * 2 + core, (y % 2) * NZ + z)

    right, left = place(z=(z + 1) % NZ), place(z=(z + NZ - 1) % NZ)
    partner = place(y=yh * 2 + 1 - yl)
    sibling = place(core=1 - core)

    def remote(src, dst, s, r, device):
        return pltpu.make_async_remote_copy(
            src_ref=src, dst_ref=dst, send_sem=s, recv_sem=r, device_id=device, device_id_type=MESH
        )

    loads = [
        pltpu.make_async_copy(hc_hbm, hx.at[TEXT, q], load_sem.at[0]),
        pltpu.make_async_copy(wc_hbm, w.at[TEXT], load_sem.at[1]),
        pltpu.make_async_copy(wv_hbm, w.at[CLIP], load_sem.at[2]),
        pltpu.make_async_copy(hv_hbm, hx.at[CLIP, q], load_sem.at[3]),
        pltpu.make_async_copy(match_hbm, match_ref, load_sem.at[4]),
        pltpu.make_async_copy(scale_hbm, scale_ref, load_sem.at[5]),
        pltpu.make_async_copy(shift_hbm, shift_ref, load_sem.at[6]),
    ]

    barrier = pltpu.get_barrier_semaphore()
    near = [right, left, sibling]
    near += [place(x=(x + o) % 4) for o in (1, 2, 3)] + [place(y=(y + o) % 4) for o in (1, 2, 3)]
    for device in near:
        pl.semaphore_signal(barrier, 1, device_id=device, device_id_type=MESH)
    loads[0].start()
    loads[1].start()

    def project(tower):
        raw = jnp.dot(hx[tower, q], w[tower], preferred_element_type=F32)
        size = jnp.sqrt(jnp.sum(raw * raw, axis=1, keepdims=True) + 1e-06)
        vec = raw * (1.0 / size)
        unit[tower] = vec
        inverse[tower] = 1.0 / size
        return vec.astype(BF16)

    def ring(d, k, c):
        first = isinstance(k, int) and k == 1
        last = isinstance(k, int) and k == 8
        src = tt.at[k - 1, pl.ds((0 if first else TOK * d) + ROWS * c, ROWS)]
        if first and c in AHEAD[d]:
            src = hx.at[TEXT, q, pl.ds(ROWS * c, ROWS)]
        dst = tt.at[k, pl.ds((0 if last else TOK * d) + ROWS * c, ROWS)]
        return remote(src, dst, ring_s.at[d, k - 1, c], ring_r.at[d, k - 1, c], (right, left)[d])

    def back(d, k, c):
        rows = pl.ds(ROWS * c, ROWS)
        return remote(
            back_out.at[d, k - 1, rows],
            back_in.at[d, k - 1, rows],
            back_s.at[d, k - 1, c],
            back_r.at[d, k - 1, c],
            (left, right)[d],
        )

    def hid_copy(tower, o, wait=False):
        index = ((x - o + 4) % 4) * 2 + core if wait else q
        return remote(
            hx.at[tower, index],
            hx.at[tower, index],
            hid_s.at[tower, o - 1],
            hid_r.at[tower, o - 1],
            place(x=(x + o) % NX),
        )

    def relay(tower, o, wait=False):
        index = ((x - o + 4) % 4) * 2 + ((1 - core) if wait else core)
        return remote(
            hx.at[tower, index], hx.at[tower, index], rel_s.at[tower, o], rel_r.at[tower, o], sibling
        )

    loads[0].wait()
    pl.semaphore_wait(barrier, len(near))
    for i in (0, 1):
        for d in (0, 1):
            ring(d, 1, AHEAD[d][i]).start()
    loads[1].wait()
    for copy in loads[2:]:
        copy.start()
    tt[0, pl.ds(0, TOK)] = project(TEXT)
    for i in (0, 1):
        for d in (0, 1):
            ring(d, 1, LATE[d][i]).start()

    def forward(k, chunks):
        for i in (0, 1):
            for d in (0, 1):
                c = chunks[d][i]
                ring(d, k, c).wait_recv()
                if not (isinstance(k, int) and k == 7 and c in AHEAD[d]):
                    ring(d, k + 1, c).start()

    forward(1, AHEAD)
    loads[2].wait()
    loads[3].wait()
    emb[pl.ds(0, TOK)] = project(CLIP)
    share_emb = remote(
        emb.at[pl.ds(0, TOK)], emb.at[pl.ds(TOK, TOK)], share_s.at[0], share_r.at[0], partner
    )
    share_emb.start()
    for tower in (CLIP, TEXT):
        for o in (1, 3, 2):
            hid_copy(tower, o).start()
        relay(tower, 0).start()

    for copy in loads[4:]:
        copy.wait()
    scale = scale_ref[0]
    shift = shift_ref[0]

    def embeddings(k):
        chunks = [tt[k, pl.ds(ROWS * c, ROWS)] for c in range(2 * NC)]
        hidden = [c for c in range(2 * NC) if c % NC in AHEAD[c // NC]]
        raw = jnp.dot(
            jnp.concatenate([chunks[c] for c in hidden], axis=0),
            w[TEXT],
            preferred_element_type=F32,
        )
        size = jnp.sqrt(jnp.sum(raw * raw, axis=1, keepdims=True) + 1e-06)
        vec = (raw * (1.0 / size)).astype(BF16)
        for i, c in enumerate(hidden):
            chunks[c] = vec[ROWS * i : ROWS * (i + 1)]
        return jnp.concatenate(chunks, axis=0)

    def work(k, rows):
        base0 = (yl * NZ + (z - k + NZ) % NZ) * TOK
        base1 = (yl * NZ + (z + k) % NZ) * TOK
        t = embeddings(k) if rows == 2 * TOK else tt[k, pl.ds(0, rows)]
        a = emb[...]
        scores = scale * lax.dot_general(
            t, a, (((1,), (1,)), ((), ())), preferred_element_type=F32
        ) + shift
        row = lax.broadcasted_iota(jnp.int32, (rows, 2 * TOK), 0)
        place_of = jnp.where(row < TOK, base0 + row, base1 + row - TOK)
        wanted = jnp.concatenate(
            [match_ref[pl.ds(blk, 1), :], match_ref[pl.ds((1 - yl) * NZ + z, 1), :]], axis=1
        )
        hit = place_of == wanted
        flipped = jnp.where(hit, scores, -scores)
        coef = (jnp.where(hit, -scale, scale) / (1.0 + jnp.exp(flipped))).astype(BF16)
        part[k, pl.ds(0, rows)] = jnp.dot(coef, a, preferred_element_type=F32)
        return lax.dot_general(coef, t, (((0,), (0,)), ((), ())), preferred_element_type=F32)

    forward(1, LATE)
    share_emb.wait_recv()
    cacc[...] = work(0, TOK)

    @pl.loop(2, 7)
    def _(k):
        forward(k, AHEAD)
        cacc[...] += work(k - 1, 2 * TOK)
        forward(k, LATE)

    def run(d, k, c):
        return part[k, pl.ds((0 if k == 8 else TOK * d) + ROWS * c, ROWS)]

    def send_fresh(d, k, c):
        back_out[d, k - 1, pl.ds(ROWS * c, ROWS)] = run(d, k, c).astype(BF16)
        back(d, k, c).start()

    def send_sum(d, k, c):
        rows = pl.ds(ROWS * c, ROWS)
        back(d, k + 1, c).wait_recv()
        back_out[d, k - 1, rows] = (run(d, k, c) + back_in[d, k, rows].astype(F32)).astype(BF16)
        back(d, k, c).start()

    forward(7, AHEAD)
    cacc[...] += work(6, 2 * TOK)
    forward(7, LATE)
    cacc[...] += work(7, 2 * TOK)

    for i in (0, 1):
        for d in (0, 1):
            send_fresh(d, 7, AHEAD[d][i])
    for i in (0, 1):
        for d in (0, 1):
            ring(d, 8, LATE[d][i]).wait_recv()
    cacc[...] += work(8, TOK)
    for i in (0, 1):
        for d in (0, 1):
            send_fresh(d, 8, LATE[d][i])

    share_out[...] = cacc[pl.ds(TOK, TOK)].astype(BF16)
    share_grad = remote(share_out, share_in, share_s.at[1], share_r.at[1], partner)
    share_grad.start()

    def ga_copy(tower, h, dx, dc, wait=False):
        to = ((x + dx) % 4) * 2 + (core + dc) % 2
        come = ((x - dx + 4) % 4) * 2 + (core + dc) % 2
        return remote(
            g_out.at[tower, h, to],
            g_in.at[tower, h, come if wait else q],
            ga_s.at[tower, h, dx * 2 + dc - 1],
            ga_r.at[tower, h, dx * 2 + dc - 1],
            place(x=(x + dx) % 4, core=(core + dc) % 2),
        )

    def yb_copy(tower, o):
        to = (y + o) % 4
        return remote(
            y_out.at[tower, to],
            y_in.at[tower, o],
            yb_s.at[tower, o - 1],
            yb_r.at[tower, o - 1],
            place(y=to),
        )

    def zc_copy(tower, o):
        to = (z + o) % NZ
        return remote(
            z_out.at[tower, to], z_in.at[tower, o], zc_s.at[tower], zc_r.at[tower], place(z=to)
        )

    def zc_all(tower):
        rest = pl.ds(1, NZ - 1)
        return remote(
            z_out.at[tower, rest], z_in.at[tower, rest], zc_s.at[tower], zc_r.at[tower], right
        )

    def fd_copy(tower, dy, dx, dc):
        to = ((yh + dy) % 2) * 8 + ((x + dx) % 4) * 2 + (core + dc) % 2
        return remote(
            f_all.at[tower, grp], f_all.at[tower, grp], fd_s.at[tower], fd_r.at[tower], (to, blk)
        )

    def fd_all(tower):
        rest = f_all.at[tower, pl.ds(0, 15)]
        return remote(rest, rest, fd_s.at[tower], fd_r.at[tower], right)

    def raw_grad(tower, h, grad):
        rows = pl.ds(HALF * h, HALF)
        vec = unit[tower, rows]
        radial = jnp.sum(vec * grad, axis=1, keepdims=True)
        raw = ((grad - vec * radial) * inverse[tower, rows]).astype(BF16)
        for j in range(8):
            g_out[tower, h, j] = raw[:, 128 * j : 128 * (j + 1)]
        for dx, dc in COLUMNS:
            ga_copy(tower, h, dx, dc).start()
        raw_out[tower, rows] = raw

    def hidden_grad(tower):
        (clip_hid, text_hid)[tower][...] = lax.dot_general(
            raw_out[tower], w[tower], (((1,), (1,)), ((), ())), preferred_element_type=F32
        ).astype(BF16)

    def turn(tower, h, *pairs):
        rows = pl.ds(HALF * h, HALF)
        for j in pairs:
            two = jnp.concatenate([hx[tower, 2 * j, rows], hx[tower, 2 * j + 1, rows]], axis=0)
            ht[tower, :, pl.ds(512 * h + 128 * j, 128)] = two.T

    def gathered(tower, h):
        g_in[tower, h, q] = g_out[tower, h, q]
        for dx, dc in COLUMNS[::-1]:
            ga_copy(tower, h, dx, dc, True).wait_recv()

    def product(tower, h, rows):
        g = g_in[tower, h].reshape(8 * HALF, 128)
        return jnp.dot(ht[tower, rows, pl.ds(512 * h, 512)], g, preferred_element_type=F32)

    def weight_first(tower):
        gathered(tower, 0)
        w_first[...] = product(tower, 0, pl.ds(0, D))

    def weight(tower, own):
        to = yl if own else 1 - yl
        rows = pl.ds(pl.multiple_of(512 * to, 512), 512)
        term = w_first[rows] + product(tower, 1, rows)
        term = term.reshape(NZ, 2, 16, 128).astype(BF16)
        for yh_to in (0, 1):
            y_out[tower, yh_to * 2 + to] = term[:, yh_to]
        for o in (2,) if own else (1, 3):
            yb_copy(tower, o).start()

    def over_y(tower):
        total = y_out[tower, y].astype(F32)
        for o in (1, 3, 2):
            yb_copy(tower, o).wait_recv()
            total = total + y_in[tower, o].astype(F32)
        z_out[tower] = total.astype(BF16)

    def send_z(tower):
        for o in (8, 7, 9, 6, 10, 5, 11, 4, 12, 3, 13, 2, 14, 1, 15):
            zc_copy(tower, o).start()

    def over_z(tower):
        z_in[tower, 0] = z_out[tower, z]
        zc_all(tower).wait_recv()
        f_all[tower, grp] = jnp.sum(z_in[tower].astype(F32), axis=0).astype(BF16)
        for dy, dx, dc in ALL_GRP:
            fd_copy(tower, dy, dx, dc).start()

    def relays(tower):
        for o in (1, 2, 3):
            hid_copy(tower, o, True).wait_recv()
            relay(tower, o).start()

    def relays_done(tower):
        for o in range(4):
            relay(tower, o, True).wait_recv()

    def clip_raw(h):
        if h == 0:
            share_grad.wait_recv()
        rows = pl.ds(HALF * h, HALF)
        raw_grad(CLIP, h, cacc[rows] + share_in[rows].astype(F32))

    def text_raw(h):
        rows = pl.ds(HALF * h, HALF)
        sums = back_in[0, 0, rows].astype(F32) + back_in[1, 0, rows].astype(F32)
        raw_grad(TEXT, h, part[0, rows] + sums)

    def ring_left(k):
        for d in (0, 1):
            for c in range(NC) if k < 8 else LATE[d]:
                ring(d, k, c).wait_send()

    def hidden_left():
        for tower in (CLIP, TEXT):
            for o in range(4):
                relay(tower, o).wait_send()
            for o in (1, 2, 3):
                hid_copy(tower, o).wait_send()

    def columns_left(tower):
        for h in (0, 1):
            for dx, dc in COLUMNS:
                ga_copy(tower, h, dx, dc).wait_send()

    def sums_left(tower):
        for o in (1, 2, 3):
            yb_copy(tower, o).wait_send()

    pieces = {
        0: lambda: relays(CLIP),
        2: lambda: ring_left(1),
        3: lambda: relays_done(CLIP),
        4: lambda: turn(CLIP, 0, 0, 1),
        5: lambda: turn(CLIP, 0, 2, 3),
        6: lambda: clip_raw(0),
        7: lambda: clip_raw(1),
        8: lambda: hidden_grad(CLIP),
        9: lambda: turn(CLIP, 1, 0, 1),
        10: lambda: turn(CLIP, 1, 2, 3),
        11: lambda: weight_first(CLIP),
        12: lambda: gathered(CLIP, 1),
        13: lambda: weight(CLIP, True),
        14: lambda: weight(CLIP, False),
        15: lambda: relays(TEXT),
        16: lambda: ring_left(2),
        17: lambda: relays_done(TEXT),
        18: lambda: turn(TEXT, 0, 0, 1),
        19: lambda: turn(TEXT, 0, 2, 3),
        20: lambda: turn(TEXT, 1, 0, 1),
        21: lambda: turn(TEXT, 1, 2, 3),
        22: lambda: over_y(CLIP),
        23: lambda: (ring_left(3), ring_left(4)),
        24: lambda: ring_left(5),
        25: lambda: (ring_left(6), ring_left(7)),
        26: lambda: ring_left(8),
    }
    for j in range(6, -1, -1):
        for i in range(4):
            for d in (0, 1):
                if i >= 2:
                    send_sum(d, j + 1, LATE[d][i - 2])
                elif j >= 1:
                    send_sum(d, j, AHEAD[d][i])
                else:
                    back(d, 1, AHEAD[d][i]).wait_recv()
            pieces.get((6 - j) * 4 + i, lambda: None)()
    for i in (0, 1):
        for d in (0, 1):
            back(d, 1, LATE[d][i]).wait_recv()
        text_raw(i)
    send_z(CLIP)
    hidden_grad(TEXT)
    weight_first(TEXT)
    gathered(TEXT, 1)
    weight(TEXT, True)
    weight(TEXT, False)
    over_y(TEXT)
    send_z(TEXT)
    over_z(CLIP)
    for d in (0, 1):
        for c in range(NC):

            @pl.loop(1, 8)
            def _(k):
                back(d, k, c).wait_send()

        for c in LATE[d]:
            back(d, 8, c).wait_send()
    fd_all(CLIP).wait()
    hidden_left()
    share_emb.wait_send()
    share_grad.wait_send()
    columns_left(CLIP)
    sums_left(CLIP)
    zc_all(CLIP).wait_send()
    over_z(TEXT)
    columns_left(TEXT)
    sums_left(TEXT)
    zc_all(TEXT).wait_send()
    fd_all(TEXT).wait()


def hand_over(clip_in, text_in, pieces, clip_hid, text_hid, clip_wg, text_wg, placed, sem):
    copies = [
        pltpu.make_async_copy(clip_in, clip_hid, sem.at[0]),
        pltpu.make_async_copy(text_in, text_hid, sem.at[1]),
        pltpu.make_async_copy(placed.at[CLIP], clip_wg, sem.at[2]),
        pltpu.make_async_copy(placed.at[TEXT], text_wg, sem.at[3]),
    ]
    copies[0].start()
    copies[1].start()
    for tower in (CLIP, TEXT):
        for j in range(16):
            rows, columns = pl.ds(16 * (j // 8), 16), pl.ds(128 * (j % 8), 128)
            placed[tower, rows, columns] = pieces[tower, j].astype(F32)
        copies[2 + tower].start()
    for copy in copies:
        copy.wait()


def local(hv, hc, wv, wc, match, multiplier, offset):
    vmem = pl.BlockSpec(memory_space=pltpu.VMEM)
    anywhere = pl.BlockSpec(memory_space=pl.ANY)
    dma = pltpu.SemaphoreType.DMA
    hidden = jax.ShapeDtypeStruct((TOK, D), BF16)
    gradient = jax.ShapeDtypeStruct((32, E), F32)
    results = pl.pallas_call(
        kernel,
        out_shape=(
            pltpu.VMEM((TOK, D), BF16),
            pltpu.VMEM((TOK, D), BF16),
            pltpu.VMEM((2, 16, 16, 128), BF16),
        ),
        in_specs=[pl.BlockSpec(memory_space=pltpu.HBM)] * 7,
        out_specs=(vmem,) * 3,
        scratch_shapes=[
            pltpu.VMEM((2, D, E), BF16),
            pltpu.VMEM((2, 8, TOK, D), BF16),
            pltpu.VMEM((2, D, 8 * TOK), BF16),
            pltpu.VMEM((2, TOK, E), F32),
            pltpu.VMEM((2, TOK, 1), F32),
            pltpu.VMEM((9, 2 * TOK, E), BF16),
            pltpu.VMEM((2 * TOK, E), BF16),
            pltpu.VMEM((9, 2 * TOK, E), F32),
            pltpu.VMEM((2 * TOK, E), F32),
            pltpu.VMEM((2, 8, TOK, E), BF16),
            pltpu.VMEM((2, 8, TOK, E), BF16),
            pltpu.VMEM((TOK, E), BF16),
            pltpu.VMEM((TOK, E), BF16),
            pltpu.VMEM((2, TOK, E), BF16),
            pltpu.VMEM((2, 2, 8, HALF, 128), BF16),
            pltpu.VMEM((2, 2, 8, HALF, 128), BF16),
            pltpu.VMEM((D, 128), F32),
            pltpu.VMEM((2, 4, NZ, 16, 128), BF16),
            pltpu.VMEM((2, 4, NZ, 16, 128), BF16),
            pltpu.VMEM((2, NZ, 16, 128), BF16),
            pltpu.VMEM((2, NZ, 16, 128), BF16),
            pltpu.VMEM((32, TOK), jnp.int32),
            pltpu.SMEM((1,), F32),
            pltpu.SMEM((1,), F32),
            dma((7,)),
            dma((2, 8, NC)),
            dma((2, 8, NC)),
            dma((2, 8, NC)),
            dma((2, 8, NC)),
            dma((2,)),
            dma((2,)),
            dma((2, 3)),
            dma((2, 3)),
            dma((2, 4)),
            dma((2, 4)),
            dma((2, 2, 7)),
            dma((2, 2, 7)),
            dma((2, 3)),
            dma((2, 3)),
            dma((2,)),
            dma((2,)),
            dma((2,)),
            dma((2,)),
        ],
        compiler_params=pltpu.CompilerParams(
            collective_id=0, has_side_effects=True, vmem_limit_bytes=56 << 20
        ),
    )(hv, hc, wv, wc, match.reshape(32, TOK), multiplier, offset)
    return pl.pallas_call(
        hand_over,
        out_shape=(hidden, hidden, gradient, gradient),
        in_specs=[vmem] * 3,
        out_specs=(anywhere,) * 4,
        scratch_shapes=[pltpu.VMEM((2, 32, E), F32), dma((4,))],
    )(*(pltpu.with_memory_space_constraint(a, pltpu.VMEM) for a in results))


def solution(mesh):
    placed = (P(("grp", "blk"), None), P(("grp", "blk"), None), P(), P(), P("grp"), P(), P())
    return jax.shard_map(
        local,
        mesh=mesh,
        in_specs=placed,
        out_specs=(
            P(("grp", "blk"), None),
            P(("grp", "blk"), None),
            P("blk", None),
            P("blk", None),
        ),
        check_vma=False,
    )
```

```python
import jax
import jax.numpy as jnp
from jax import lax
from jax.experimental import pallas as pl
from jax.experimental.pallas import tpu as pltpu
from jax.sharding import PartitionSpec as P

MESH = pl.DeviceIdType.MESH
F32 = jnp.float32
BF16 = jnp.bfloat16
NX, NZ, TOK, D, E = 4, 16, 128, 1024, 1024
NC = 4
ROWS = TOK // NC
HALF = TOK // 2
LATE = ((0, 2), (1, 3))
AHEAD = ((1, 3), (0, 2))
COLUMNS = ((2, 1), (2, 0), (1, 1), (3, 1), (1, 0), (3, 0), (0, 1))
ALL_GRP = tuple((1,) + p for p in COLUMNS) + ((1, 0, 0),) + tuple((0,) + p for p in COLUMNS)
CLIP, TEXT = 0, 1


def kernel(
    hv_hbm,
    hc_hbm,
    wv_hbm,
    wc_hbm,
    match_hbm,
    scale_hbm,
    shift_hbm,
    clip_hid,
    text_hid,
    f_all,
    w,
    hx,
    ht,
    unit,
    inverse,
    tt,
    emb,
    part,
    cacc,
    back_in,
    back_out,
    share_out,
    share_in,
    raw_out,
    g_out,
    g_in,
    w_first,
    y_out,
    y_in,
    z_out,
    z_in,
    match_ref,
    scale_ref,
    shift_ref,
    load_sem,
    ring_s,
    ring_r,
    back_s,
    back_r,
    share_s,
    share_r,
    hid_s,
    hid_r,
    rel_s,
    rel_r,
    ga_s,
    ga_r,
    yb_s,
    yb_r,
    zc_s,
    zc_r,
    fd_s,
    fd_r,
):
    grp = lax.axis_index("grp")
    blk = lax.axis_index("blk")
    yh, x, core = grp // 8, (grp // 2) % 4, grp % 2
    yl, z = blk // NZ, blk % NZ
    y = yh * 2 + yl
    q = x * 2 + core

    def place(x=x, y=y, z=z, core=core):
        return ((y // 2) * 8 + x * 2 + core, (y % 2) * NZ + z)

    right, left = place(z=(z + 1) % NZ), place(z=(z + NZ - 1) % NZ)
    partner = place(y=yh * 2 + 1 - yl)
    sibling = place(core=1 - core)

    def remote(src, dst, s, r, device):
        return pltpu.make_async_remote_copy(
            src_ref=src, dst_ref=dst, send_sem=s, recv_sem=r, device_id=device, device_id_type=MESH
        )

    loads = [
        pltpu.make_async_copy(hc_hbm, hx.at[TEXT, q], load_sem.at[0]),
        pltpu.make_async_copy(wc_hbm, w.at[TEXT], load_sem.at[1]),
        pltpu.make_async_copy(wv_hbm, w.at[CLIP], load_sem.at[2]),
        pltpu.make_async_copy(hv_hbm, hx.at[CLIP, q], load_sem.at[3]),
        pltpu.make_async_copy(match_hbm, match_ref, load_sem.at[4]),
        pltpu.make_async_copy(scale_hbm, scale_ref, load_sem.at[5]),
        pltpu.make_async_copy(shift_hbm, shift_ref, load_sem.at[6]),
    ]

    barrier = pltpu.get_barrier_semaphore()
    near = [right, left, sibling]
    near += [place(x=(x + o) % 4) for o in (1, 2, 3)] + [place(y=(y + o) % 4) for o in (1, 2, 3)]
    for device in near:
        pl.semaphore_signal(barrier, 1, device_id=device, device_id_type=MESH)
    loads[0].start()
    loads[1].start()

    def project(tower):
        raw = jnp.dot(hx[tower, q], w[tower], preferred_element_type=F32)
        size = jnp.sqrt(jnp.sum(raw * raw, axis=1, keepdims=True) + 1e-06)
        vec = raw * (1.0 / size)
        unit[tower] = vec
        inverse[tower] = 1.0 / size
        return vec.astype(BF16)

    def ring(d, k, c):
        first = isinstance(k, int) and k == 1
        last = isinstance(k, int) and k == 8
        src = tt.at[k - 1, pl.ds((0 if first else TOK * d) + ROWS * c, ROWS)]
        if first and c in AHEAD[d]:
            src = hx.at[TEXT, q, pl.ds(ROWS * c, ROWS)]
        dst = tt.at[k, pl.ds((0 if last else TOK * d) + ROWS * c, ROWS)]
        return remote(src, dst, ring_s.at[d], ring_r.at[d, k - 1, c], (right, left)[d])

    def back(d, k, c):
        rows = pl.ds(ROWS * c, ROWS)
        return remote(
            back_out.at[d, k - 1, rows],
            back_in.at[d, k - 1, rows],
            back_s.at[d],
            back_r.at[d, k - 1, c],
            (left, right)[d],
        )

    def hid_copy(tower, o):
        return remote(
            hx.at[tower, q],
            hx.at[tower, q],
            hid_s.at[tower],
            hid_r.at[tower],
            place(x=(x + o) % NX),
        )

    def relay(tower, o):
        index = ((x - o + 4) % 4) * 2 + core
        return remote(
            hx.at[tower, index], hx.at[tower, index], rel_s.at[tower], rel_r.at[tower], sibling
        )

    def ring_all(d, sems):
        chunks = tt.at[pl.ds(0, 5), pl.ds(0, 192)]
        return remote(chunks, chunks, sems.at[d], ring_r.at[d, 0, 0], right)

    def hid_all(tower):
        blocks = hx.at[tower, pl.ds(0, 3)]
        return remote(blocks, blocks, hid_s.at[tower], hid_r.at[tower], right)

    def relay_all(tower):
        blocks = hx.at[tower, pl.ds(0, 4)]
        return remote(blocks, blocks, rel_s.at[tower], rel_r.at[tower], sibling)

    loads[0].wait()
    pl.semaphore_wait(barrier, len(near))
    for i in (0, 1):
        for d in (0, 1):
            ring(d, 1, AHEAD[d][i]).start()
    loads[1].wait()
    for copy in loads[2:]:
        copy.start()
    tt[0, pl.ds(0, TOK)] = project(TEXT)
    for i in (0, 1):
        for d in (0, 1):
            ring(d, 1, LATE[d][i]).start()

    def forward(k, chunks):
        for i in (0, 1):
            for d in (0, 1):
                c = chunks[d][i]
                ring(d, k, c).wait_recv()
                if not (isinstance(k, int) and k == 7 and c in AHEAD[d]):
                    ring(d, k + 1, c).start()

    forward(1, AHEAD)
    loads[2].wait()
    loads[3].wait()
    emb[pl.ds(0, TOK)] = project(CLIP)
    share_emb = remote(
        emb.at[pl.ds(0, TOK)], emb.at[pl.ds(TOK, TOK)], share_s.at[0], share_r.at[0], partner
    )
    share_emb.start()
    for tower in (CLIP, TEXT):
        for o in (1, 3, 2):
            hid_copy(tower, o).start()
        relay(tower, 0).start()

    for copy in loads[4:]:
        copy.wait()
    scale = scale_ref[0]
    shift = shift_ref[0]

    def embeddings(k):
        chunks = [tt[k, pl.ds(ROWS * c, ROWS)] for c in range(2 * NC)]
        hidden = [c for c in range(2 * NC) if c % NC in AHEAD[c // NC]]
        raw = jnp.dot(
            jnp.concatenate([chunks[c] for c in hidden], axis=0),
            w[TEXT],
            preferred_element_type=F32,
        )
        size = jnp.sqrt(jnp.sum(raw * raw, axis=1, keepdims=True) + 1e-06)
        vec = (raw * (1.0 / size)).astype(BF16)
        for i, c in enumerate(hidden):
            chunks[c] = vec[ROWS * i : ROWS * (i + 1)]
        return jnp.concatenate(chunks, axis=0)

    def work(k, rows):
        base0 = (yl * NZ + (z - k + NZ) % NZ) * TOK
        base1 = (yl * NZ + (z + k) % NZ) * TOK
        t = embeddings(k) if rows == 2 * TOK else tt[k, pl.ds(0, rows)]
        a = emb[...]
        scores = scale * lax.dot_general(
            t, a, (((1,), (1,)), ((), ())), preferred_element_type=F32
        ) + shift
        row = lax.broadcasted_iota(jnp.int32, (rows, 2 * TOK), 0)
        place_of = jnp.where(row < TOK, base0 + row, base1 + row - TOK)
        wanted = jnp.concatenate(
            [match_ref[pl.ds(blk, 1), :], match_ref[pl.ds((1 - yl) * NZ + z, 1), :]], axis=1
        )
        hit = place_of == wanted
        flipped = jnp.where(hit, scores, -scores)
        coef = (jnp.where(hit, -scale, scale) / (1.0 + jnp.exp(flipped))).astype(BF16)
        part[k, pl.ds(0, rows)] = jnp.dot(coef, a, preferred_element_type=F32)
        return lax.dot_general(coef, t, (((0,), (0,)), ((), ())), preferred_element_type=F32)

    forward(1, LATE)
    share_emb.wait_recv()
    cacc[...] = work(0, TOK)

    @pl.loop(2, 7)
    def _(k):
        forward(k, AHEAD)
        cacc[...] += work(k - 1, 2 * TOK)
        forward(k, LATE)

    def run(d, k, c):
        return part[k, pl.ds((0 if k == 8 else TOK * d) + ROWS * c, ROWS)]

    def send_fresh(d, k, c):
        back_out[d, k - 1, pl.ds(ROWS * c, ROWS)] = run(d, k, c).astype(BF16)
        back(d, k, c).start()

    def send_sum(d, k, c):
        rows = pl.ds(ROWS * c, ROWS)
        back(d, k + 1, c).wait_recv()
        back_out[d, k - 1, rows] = (run(d, k, c) + back_in[d, k, rows].astype(F32)).astype(BF16)
        back(d, k, c).start()

    forward(7, AHEAD)
    cacc[...] += work(6, 2 * TOK)
    forward(7, LATE)
    cacc[...] += work(7, 2 * TOK)

    for i in (0, 1):
        for d in (0, 1):
            send_fresh(d, 7, AHEAD[d][i])
    for i in (0, 1):
        for d in (0, 1):
            ring(d, 8, LATE[d][i]).wait_recv()
    cacc[...] += work(8, TOK)
    for i in (0, 1):
        for d in (0, 1):
            send_fresh(d, 8, LATE[d][i])

    share_out[...] = cacc[pl.ds(TOK, TOK)].astype(BF16)
    share_grad = remote(share_out, share_in, share_s.at[1], share_r.at[1], partner)
    share_grad.start()

    def ga_copy(tower, h, dx, dc):
        to = ((x + dx) % 4) * 2 + (core + dc) % 2
        return remote(
            g_out.at[tower, h, to],
            g_in.at[tower, h, q],
            ga_s.at[tower],
            ga_r.at[tower, h],
            place(x=(x + dx) % 4, core=(core + dc) % 2),
        )

    def yb_copy(tower, o):
        to = (y + o) % 4
        return remote(
            y_out.at[tower, to], y_in.at[tower, o], yb_s.at[tower], yb_r.at[tower], place(y=to)
        )

    def ga_half(tower, h):
        parts = g_in.at[tower, h, pl.ds(0, 7)]
        return remote(parts, parts, ga_s.at[tower], ga_r.at[tower, h], sibling)

    def ga_both(tower):
        parts = g_out.at[tower, :, pl.ds(0, 7)]
        return remote(parts, parts, ga_s.at[tower], ga_r.at[tower, 0], sibling)

    def yb_all(tower):
        rest = pl.ds(1, 3)
        return remote(
            y_out.at[tower, rest], y_in.at[tower, rest], yb_s.at[tower], yb_r.at[tower], partner
        )

    def zc_copy(tower, o):
        to = (z + o) % NZ
        return remote(
            z_out.at[tower, to], z_in.at[tower, o], zc_s.at[tower], zc_r.at[tower], place(z=to)
        )

    def zc_all(tower):
        rest = pl.ds(1, NZ - 1)
        return remote(
            z_out.at[tower, rest], z_in.at[tower, rest], zc_s.at[tower], zc_r.at[tower], right
        )

    def fd_copy(tower, dy, dx, dc):
        to = ((yh + dy) % 2) * 8 + ((x + dx) % 4) * 2 + (core + dc) % 2
        return remote(
            f_all.at[tower, grp], f_all.at[tower, grp], fd_s.at[tower], fd_r.at[tower], (to, blk)
        )

    def fd_all(tower):
        rest = f_all.at[tower, pl.ds(0, 15)]
        return remote(rest, rest, fd_s.at[tower], fd_r.at[tower], right)

    def raw_grad(tower, h, grad):
        rows = pl.ds(HALF * h, HALF)
        vec = unit[tower, rows]
        radial = jnp.sum(vec * grad, axis=1, keepdims=True)
        raw = ((grad - vec * radial) * inverse[tower, rows]).astype(BF16)
        for j in range(8):
            g_out[tower, h, j] = raw[:, 128 * j : 128 * (j + 1)]
        for dx, dc in COLUMNS:
            ga_copy(tower, h, dx, dc).start()
        raw_out[tower, rows] = raw

    def hidden_grad(tower):
        (clip_hid, text_hid)[tower][...] = lax.dot_general(
            raw_out[tower], w[tower], (((1,), (1,)), ((), ())), preferred_element_type=F32
        ).astype(BF16)

    def turn(tower, h, *pairs):
        rows = pl.ds(HALF * h, HALF)
        for j in pairs:
            two = jnp.concatenate([hx[tower, 2 * j, rows], hx[tower, 2 * j + 1, rows]], axis=0)
            ht[tower, :, pl.ds(512 * h + 128 * j, 128)] = two.T

    def gathered(tower, h):
        g_in[tower, h, q] = g_out[tower, h, q]
        ga_half(tower, h).wait_recv()

    def product(tower, h, rows):
        g = g_in[tower, h].reshape(8 * HALF, 128)
        return jnp.dot(ht[tower, rows, pl.ds(512 * h, 512)], g, preferred_element_type=F32)

    def weight_first(tower):
        gathered(tower, 0)
        w_first[...] = product(tower, 0, pl.ds(0, D))

    def weight(tower, own):
        to = yl if own else 1 - yl
        rows = pl.ds(pl.multiple_of(512 * to, 512), 512)
        term = w_first[rows] + product(tower, 1, rows)
        term = term.reshape(NZ, 2, 16, 128).astype(BF16)
        for yh_to in (0, 1):
            y_out[tower, yh_to * 2 + to] = term[:, yh_to]
        for o in (2,) if own else (1, 3):
            yb_copy(tower, o).start()

    def over_y(tower):
        yb_all(tower).wait_recv()
        total = y_out[tower, y].astype(F32)
        for o in (1, 2, 3):
            total = total + y_in[tower, o].astype(F32)
        z_out[tower] = total.astype(BF16)

    def send_z(tower):
        for o in (8, 7, 9, 6, 10, 5, 11, 4, 12, 3, 13, 2, 14, 1, 15):
            zc_copy(tower, o).start()

    def over_z(tower):
        z_in[tower, 0] = z_out[tower, z]
        zc_all(tower).wait_recv()
        f_all[tower, grp] = jnp.sum(z_in[tower].astype(F32), axis=0).astype(BF16)
        for dy, dx, dc in ALL_GRP:
            fd_copy(tower, dy, dx, dc).start()

    def relays(tower):
        hid_all(tower).wait_recv()
        for o in (1, 2, 3):
            relay(tower, o).start()

    def clip_raw(h):
        if h == 0:
            share_grad.wait_recv()
        rows = pl.ds(HALF * h, HALF)
        raw_grad(CLIP, h, cacc[rows] + share_in[rows].astype(F32))

    def text_raw(h):
        rows = pl.ds(HALF * h, HALF)
        sums = back_in[0, 0, rows].astype(F32) + back_in[1, 0, rows].astype(F32)
        raw_grad(TEXT, h, part[0, rows] + sums)

    pieces = {
        0: lambda: relays(CLIP),
        3: lambda: relay_all(CLIP).wait_recv(),
        4: lambda: turn(CLIP, 0, 0, 1),
        5: lambda: turn(CLIP, 0, 2, 3),
        6: lambda: clip_raw(0),
        7: lambda: clip_raw(1),
        8: lambda: hidden_grad(CLIP),
        9: lambda: turn(CLIP, 1, 0, 1),
        10: lambda: turn(CLIP, 1, 2, 3),
        11: lambda: weight_first(CLIP),
        12: lambda: gathered(CLIP, 1),
        13: lambda: weight(CLIP, True),
        14: lambda: weight(CLIP, False),
        15: lambda: relays(TEXT),
        17: lambda: relay_all(TEXT).wait_recv(),
        18: lambda: turn(TEXT, 0, 0, 1),
        19: lambda: turn(TEXT, 0, 2, 3),
        20: lambda: turn(TEXT, 1, 0, 1),
        21: lambda: turn(TEXT, 1, 2, 3),
        22: lambda: over_y(CLIP),
        24: lambda: ring_all(0, ring_s).wait_send(),
        25: lambda: ring_all(1, ring_s).wait_send(),
    }
    for j in range(6, -1, -1):
        for i in range(4):
            for d in (0, 1):
                if i >= 2:
                    send_sum(d, j + 1, LATE[d][i - 2])
                elif j >= 1:
                    send_sum(d, j, AHEAD[d][i])
                else:
                    back(d, 1, AHEAD[d][i]).wait_recv()
            pieces.get((6 - j) * 4 + i, lambda: None)()
    for i in (0, 1):
        for d in (0, 1):
            back(d, 1, LATE[d][i]).wait_recv()
        text_raw(i)
    send_z(CLIP)
    hidden_grad(TEXT)
    weight_first(TEXT)
    gathered(TEXT, 1)
    weight(TEXT, True)
    weight(TEXT, False)
    over_y(TEXT)
    send_z(TEXT)
    over_z(CLIP)
    for d in (0, 1):
        ring_all(d, back_s).wait_send()
    share_emb.wait_send()
    share_grad.wait_send()
    for tower in (CLIP, TEXT):
        hid_all(tower).wait_send()
        relay_all(tower).wait_send()
        ga_both(tower).wait_send()
        yb_all(tower).wait_send()
    zc_all(CLIP).wait_send()
    over_z(TEXT)
    zc_all(TEXT).wait_send()
    fd_all(CLIP).wait()
    fd_all(TEXT).wait()


def hand_over(clip_in, text_in, pieces, clip_hid, text_hid, clip_wg, text_wg, placed, sem):
    copies = [
        pltpu.make_async_copy(clip_in, clip_hid, sem.at[0]),
        pltpu.make_async_copy(text_in, text_hid, sem.at[1]),
        pltpu.make_async_copy(placed.at[CLIP], clip_wg, sem.at[2]),
        pltpu.make_async_copy(placed.at[TEXT], text_wg, sem.at[3]),
    ]
    copies[0].start()
    copies[1].start()
    for tower in (CLIP, TEXT):
        for j in range(16):
            rows, columns = pl.ds(16 * (j // 8), 16), pl.ds(128 * (j % 8), 128)
            placed[tower, rows, columns] = pieces[tower, j].astype(F32)
        copies[2 + tower].start()
    for copy in copies:
        copy.wait()


def local(hv, hc, wv, wc, match, multiplier, offset):
    vmem = pl.BlockSpec(memory_space=pltpu.VMEM)
    anywhere = pl.BlockSpec(memory_space=pl.ANY)
    dma = pltpu.SemaphoreType.DMA
    hidden = jax.ShapeDtypeStruct((TOK, D), BF16)
    gradient = jax.ShapeDtypeStruct((32, E), F32)
    results = pl.pallas_call(
        kernel,
        out_shape=(
            pltpu.VMEM((TOK, D), BF16),
            pltpu.VMEM((TOK, D), BF16),
            pltpu.VMEM((2, 16, 16, 128), BF16),
        ),
        in_specs=[pl.BlockSpec(memory_space=pltpu.HBM)] * 7,
        out_specs=(vmem,) * 3,
        scratch_shapes=[
            pltpu.VMEM((2, D, E), BF16),
            pltpu.VMEM((2, 8, TOK, D), BF16),
            pltpu.VMEM((2, D, 8 * TOK), BF16),
            pltpu.VMEM((2, TOK, E), F32),
            pltpu.VMEM((2, TOK, 1), F32),
            pltpu.VMEM((9, 2 * TOK, E), BF16),
            pltpu.VMEM((2 * TOK, E), BF16),
            pltpu.VMEM((9, 2 * TOK, E), F32),
            pltpu.VMEM((2 * TOK, E), F32),
            pltpu.VMEM((2, 8, TOK, E), BF16),
            pltpu.VMEM((2, 8, TOK, E), BF16),
            pltpu.VMEM((TOK, E), BF16),
            pltpu.VMEM((TOK, E), BF16),
            pltpu.VMEM((2, TOK, E), BF16),
            pltpu.VMEM((2, 2, 8, HALF, 128), BF16),
            pltpu.VMEM((2, 2, 8, HALF, 128), BF16),
            pltpu.VMEM((D, 128), F32),
            pltpu.VMEM((2, 4, NZ, 16, 128), BF16),
            pltpu.VMEM((2, 4, NZ, 16, 128), BF16),
            pltpu.VMEM((2, NZ, 16, 128), BF16),
            pltpu.VMEM((2, NZ, 16, 128), BF16),
            pltpu.VMEM((32, TOK), jnp.int32),
            pltpu.SMEM((1,), F32),
            pltpu.SMEM((1,), F32),
            dma((7,)),
            dma((2,)),
            dma((2, 8, NC)),
            dma((2,)),
            dma((2, 8, NC)),
            dma((2,)),
            dma((2,)),
            dma((2,)),
            dma((2,)),
            dma((2,)),
            dma((2,)),
            dma((2,)),
            dma((2, 2)),
            dma((2,)),
            dma((2,)),
            dma((2,)),
            dma((2,)),
            dma((2,)),
            dma((2,)),
        ],
        compiler_params=pltpu.CompilerParams(
            collective_id=0, has_side_effects=True, vmem_limit_bytes=56 << 20
        ),
    )(hv, hc, wv, wc, match.reshape(32, TOK), multiplier, offset)
    return pl.pallas_call(
        hand_over,
        out_shape=(hidden, hidden, gradient, gradient),
        in_specs=[vmem] * 3,
        out_specs=(anywhere,) * 4,
        scratch_shapes=[pltpu.VMEM((2, 32, E), F32), dma((4,))],
    )(*(pltpu.with_memory_space_constraint(a, pltpu.VMEM) for a in results))


def solution(mesh):
    placed = (P(("grp", "blk"), None), P(("grp", "blk"), None), P(), P(), P("grp"), P(), P())
    return jax.shard_map(
        local,
        mesh=mesh,
        in_specs=placed,
        out_specs=(
            P(("grp", "blk"), None),
            P(("grp", "blk"), None),
            P("blk", None),
            P("blk", None),
        ),
        check_vma=False,
    )
```

```python
import jax
import jax.numpy as jnp
from jax import lax
from jax.experimental import pallas as pl
from jax.experimental.pallas import tpu as pltpu
from jax.sharding import PartitionSpec as P

MESH = pl.DeviceIdType.MESH
F32 = jnp.float32
BF16 = jnp.bfloat16
NX, NZ, TOK, D, E = 4, 16, 128, 1024, 1024
NC = 4
ROWS = TOK // NC
HALF = TOK // 2
LATE = ((0, 2), (1, 3))
AHEAD = ((1, 3), (0, 2))
COLUMNS = ((2, 1), (2, 0), (1, 1), (3, 1), (1, 0), (3, 0), (0, 1))
ALL_GRP = tuple((1,) + p for p in COLUMNS) + ((1, 0, 0),) + tuple((0,) + p for p in COLUMNS)
CLIP, TEXT = 0, 1
NEAR, FAR = 0, 1
FAR_OFFSETS = (8, 7, 9, 6, 10, 5, 11, 4)
NEAR_OFFSETS = (12, 3, 13, 2, 14, 1, 15)


def kernel(
    hv_hbm,
    hc_hbm,
    wv_hbm,
    wc_hbm,
    match_hbm,
    scale_hbm,
    shift_hbm,
    clip_hid,
    text_hid,
    f_all,
    w,
    hx,
    ht,
    unit,
    inverse,
    tt,
    emb,
    part,
    cacc,
    back_in,
    back_out,
    share_out,
    share_in,
    raw_out,
    g_out,
    g_in,
    w_first,
    y_out,
    y_in,
    z_out,
    z_in,
    match_ref,
    scale_ref,
    shift_ref,
    load_sem,
    ring_s,
    ring_r,
    back_s,
    back_r,
    share_s,
    share_r,
    hid_s,
    hid_r,
    rel_s,
    rel_r,
    ga_s,
    ga_r,
    yb_s,
    yb_r,
    zc_s,
    zc_r,
    fd_s,
    fd_r,
):
    grp = lax.axis_index("grp")
    blk = lax.axis_index("blk")
    yh, x, core = grp // 8, (grp // 2) % 4, grp % 2
    yl, z = blk // NZ, blk % NZ
    y = yh * 2 + yl
    q = x * 2 + core

    def place(x=x, y=y, z=z, core=core):
        return ((y // 2) * 8 + x * 2 + core, (y % 2) * NZ + z)

    right, left = place(z=(z + 1) % NZ), place(z=(z + NZ - 1) % NZ)
    partner = place(y=yh * 2 + 1 - yl)
    sibling = place(core=1 - core)

    def remote(src, dst, s, r, device):
        return pltpu.make_async_remote_copy(
            src_ref=src, dst_ref=dst, send_sem=s, recv_sem=r, device_id=device, device_id_type=MESH
        )

    loads = [
        pltpu.make_async_copy(hc_hbm, hx.at[TEXT, q], load_sem.at[0]),
        pltpu.make_async_copy(wc_hbm, w.at[TEXT], load_sem.at[1]),
        pltpu.make_async_copy(wv_hbm, w.at[CLIP], load_sem.at[2]),
        pltpu.make_async_copy(hv_hbm, hx.at[CLIP, q], load_sem.at[3]),
        pltpu.make_async_copy(match_hbm, match_ref, load_sem.at[4]),
        pltpu.make_async_copy(scale_hbm, scale_ref, load_sem.at[5]),
        pltpu.make_async_copy(shift_hbm, shift_ref, load_sem.at[6]),
    ]

    barrier = pltpu.get_barrier_semaphore()
    near = [right, left, sibling]
    near += [place(x=(x + o) % 4) for o in (1, 2, 3)] + [place(y=(y + o) % 4) for o in (1, 2, 3)]
    for device in near:
        pl.semaphore_signal(barrier, 1, device_id=device, device_id_type=MESH)
    loads[0].start()
    loads[1].start()

    def project(tower):
        raw = jnp.dot(hx[tower, q], w[tower], preferred_element_type=F32)
        size = jnp.sqrt(jnp.sum(raw * raw, axis=1, keepdims=True) + 1e-06)
        vec = raw * (1.0 / size)
        unit[tower] = vec
        inverse[tower] = 1.0 / size
        return vec.astype(BF16)

    def ring(d, k, c):
        first = isinstance(k, int) and k == 1
        last = isinstance(k, int) and k == 8
        src = tt.at[k - 1, pl.ds((0 if first else TOK * d) + ROWS * c, ROWS)]
        if first and c in AHEAD[d]:
            src = hx.at[TEXT, q, pl.ds(ROWS * c, ROWS)]
        dst = tt.at[k, pl.ds((0 if last else TOK * d) + ROWS * c, ROWS)]
        return remote(src, dst, ring_s.at[d], ring_r.at[d, k - 1, c], (right, left)[d])

    def back(d, k, c):
        rows = pl.ds(ROWS * c, ROWS)
        return remote(
            back_out.at[d, k - 1, rows],
            back_in.at[d, k - 1, rows],
            back_s.at[d],
            back_r.at[d, k - 1, c],
            (left, right)[d],
        )

    def hid_copy(tower, o):
        return remote(
            hx.at[tower, q],
            hx.at[tower, q],
            hid_s.at[tower],
            hid_r.at[tower],
            place(x=(x + o) % NX),
        )

    def relay(tower, o):
        index = ((x - o + 4) % 4) * 2 + core
        return remote(
            hx.at[tower, index], hx.at[tower, index], rel_s.at[tower], rel_r.at[tower], sibling
        )

    def ring_all(d, sems):
        chunks = tt.at[pl.ds(0, 5), pl.ds(0, 192)]
        return remote(chunks, chunks, sems.at[d], ring_r.at[d, 0, 0], right)

    def hid_all(tower):
        blocks = hx.at[tower, pl.ds(0, 3)]
        return remote(blocks, blocks, hid_s.at[tower], hid_r.at[tower], right)

    def relay_all(tower):
        blocks = hx.at[tower, pl.ds(0, 4)]
        return remote(blocks, blocks, rel_s.at[tower], rel_r.at[tower], sibling)

    loads[0].wait()
    pl.semaphore_wait(barrier, len(near))
    for i in (0, 1):
        for d in (0, 1):
            ring(d, 1, AHEAD[d][i]).start()
    loads[1].wait()
    for copy in loads[2:]:
        copy.start()
    tt[0, pl.ds(0, TOK)] = project(TEXT)
    for i in (0, 1):
        for d in (0, 1):
            ring(d, 1, LATE[d][i]).start()

    def forward(k, chunks):
        for i in (0, 1):
            for d in (0, 1):
                c = chunks[d][i]
                ring(d, k, c).wait_recv()
                if not (isinstance(k, int) and k == 7 and c in AHEAD[d]):
                    ring(d, k + 1, c).start()

    forward(1, AHEAD)
    loads[2].wait()
    loads[3].wait()
    emb[pl.ds(0, TOK)] = project(CLIP)
    share_emb = remote(
        emb.at[pl.ds(0, TOK)], emb.at[pl.ds(TOK, TOK)], share_s.at[0], share_r.at[0], partner
    )
    share_emb.start()
    for tower in (CLIP, TEXT):
        for o in (1, 3, 2):
            hid_copy(tower, o).start()
        relay(tower, 0).start()

    for copy in loads[4:]:
        copy.wait()
    scale = scale_ref[0]
    shift = shift_ref[0]

    def embeddings(k):
        chunks = [tt[k, pl.ds(ROWS * c, ROWS)] for c in range(2 * NC)]
        hidden = [c for c in range(2 * NC) if c % NC in AHEAD[c // NC]]
        raw = jnp.dot(
            jnp.concatenate([chunks[c] for c in hidden], axis=0),
            w[TEXT],
            preferred_element_type=F32,
        )
        size = jnp.sqrt(jnp.sum(raw * raw, axis=1, keepdims=True) + 1e-06)
        vec = (raw * (1.0 / size)).astype(BF16)
        for i, c in enumerate(hidden):
            chunks[c] = vec[ROWS * i : ROWS * (i + 1)]
        return jnp.concatenate(chunks, axis=0)

    def work(k, rows):
        base0 = (yl * NZ + (z - k + NZ) % NZ) * TOK
        base1 = (yl * NZ + (z + k) % NZ) * TOK
        t = embeddings(k) if rows == 2 * TOK else tt[k, pl.ds(0, rows)]
        a = emb[...]
        scores = scale * lax.dot_general(
            t, a, (((1,), (1,)), ((), ())), preferred_element_type=F32
        ) + shift
        row = lax.broadcasted_iota(jnp.int32, (rows, 2 * TOK), 0)
        place_of = jnp.where(row < TOK, base0 + row, base1 + row - TOK)
        wanted = jnp.concatenate(
            [match_ref[pl.ds(blk, 1), :], match_ref[pl.ds((1 - yl) * NZ + z, 1), :]], axis=1
        )
        hit = place_of == wanted
        flipped = jnp.where(hit, scores, -scores)
        coef = (jnp.where(hit, -scale, scale) / (1.0 + jnp.exp(flipped))).astype(BF16)
        part[k, pl.ds(0, rows)] = jnp.dot(coef, a, preferred_element_type=F32)
        return lax.dot_general(coef, t, (((0,), (0,)), ((), ())), preferred_element_type=F32)

    forward(1, LATE)
    share_emb.wait_recv()
    cacc[...] = work(0, TOK)

    @pl.loop(2, 7)
    def _(k):
        forward(k, AHEAD)
        cacc[...] += work(k - 1, 2 * TOK)
        forward(k, LATE)

    def run(d, k, c):
        return part[k, pl.ds((0 if k == 8 else TOK * d) + ROWS * c, ROWS)]

    def send_fresh(d, k, c):
        back_out[d, k - 1, pl.ds(ROWS * c, ROWS)] = run(d, k, c).astype(BF16)
        back(d, k, c).start()

    def send_sum(d, k, c):
        rows = pl.ds(ROWS * c, ROWS)
        back(d, k + 1, c).wait_recv()
        back_out[d, k - 1, rows] = (run(d, k, c) + back_in[d, k, rows].astype(F32)).astype(BF16)
        back(d, k, c).start()

    forward(7, AHEAD)
    cacc[...] += work(6, 2 * TOK)
    forward(7, LATE)
    cacc[...] += work(7, 2 * TOK)

    for i in (0, 1):
        for d in (0, 1):
            send_fresh(d, 7, AHEAD[d][i])
    for i in (0, 1):
        for d in (0, 1):
            ring(d, 8, LATE[d][i]).wait_recv()
    cacc[...] += work(8, TOK)
    for i in (0, 1):
        for d in (0, 1):
            send_fresh(d, 8, LATE[d][i])

    share_out[...] = cacc[pl.ds(TOK, TOK)].astype(BF16)
    share_grad = remote(share_out, share_in, share_s.at[1], share_r.at[1], partner)
    share_grad.start()

    def ga_copy(tower, h, dx, dc):
        to = ((x + dx) % 4) * 2 + (core + dc) % 2
        return remote(
            g_out.at[tower, h, to],
            g_in.at[tower, h, q],
            ga_s.at[tower],
            ga_r.at[tower, h],
            place(x=(x + dx) % 4, core=(core + dc) % 2),
        )

    def yb_copy(tower, side, o):
        to = (y + o) % 4
        return remote(
            y_out.at[tower, side, to],
            y_in.at[tower, side, o],
            yb_s.at[tower],
            yb_r.at[tower, side],
            place(y=to),
        )

    def ga_half(tower, h):
        parts = g_in.at[tower, h, pl.ds(0, 7)]
        return remote(parts, parts, ga_s.at[tower], ga_r.at[tower, h], sibling)

    def ga_both(tower):
        parts = g_out.at[tower, :, pl.ds(0, 7)]
        return remote(parts, parts, ga_s.at[tower], ga_r.at[tower, 0], sibling)

    def yb_side(tower, side):
        parts = y_in.at[tower, side, pl.ds(1, 3)]
        return remote(parts, parts, yb_s.at[tower], yb_r.at[tower, side], partner)

    def yb_both(tower):
        parts = y_out.at[tower, :, pl.ds(0, 3)]
        return remote(parts, parts, yb_s.at[tower], yb_r.at[tower, 0], partner)

    def zc_copy(tower, o):
        to = (z + o) % NZ
        return remote(
            z_out.at[tower, (o + 4) % NZ], z_in.at[tower, o], zc_s.at[tower], zc_r.at[tower], place(z=to)
        )

    def zc_all(tower):
        rest = pl.ds(1, NZ - 1)
        return remote(
            z_out.at[tower, rest], z_in.at[tower, rest], zc_s.at[tower], zc_r.at[tower], right
        )

    def fd_copy(tower, dy, dx, dc):
        to = ((yh + dy) % 2) * 8 + ((x + dx) % 4) * 2 + (core + dc) % 2
        return remote(
            f_all.at[tower, grp], f_all.at[tower, grp], fd_s.at[tower], fd_r.at[tower], (to, blk)
        )

    def fd_all(tower):
        rest = f_all.at[tower, pl.ds(0, 15)]
        return remote(rest, rest, fd_s.at[tower], fd_r.at[tower], right)

    def raw_grad(tower, h, grad):
        rows = pl.ds(HALF * h, HALF)
        vec = unit[tower, rows]
        radial = jnp.sum(vec * grad, axis=1, keepdims=True)
        raw = ((grad - vec * radial) * inverse[tower, rows]).astype(BF16)
        for j in range(8):
            g_out[tower, h, j] = raw[:, 128 * j : 128 * (j + 1)]
        for dx, dc in COLUMNS:
            ga_copy(tower, h, dx, dc).start()
        raw_out[tower, rows] = raw

    def hidden_grad(tower):
        (clip_hid, text_hid)[tower][...] = lax.dot_general(
            raw_out[tower], w[tower], (((1,), (1,)), ((), ())), preferred_element_type=F32
        ).astype(BF16)

    def turn(tower, h, *pairs):
        rows = pl.ds(HALF * h, HALF)
        for j in pairs:
            two = jnp.concatenate([hx[tower, 2 * j, rows], hx[tower, 2 * j + 1, rows]], axis=0)
            turned = two.T.reshape(2, NZ, 2, 16, 128)
            columns = pl.ds(512 * h + 128 * j, 128)
            for z_to in range(NZ):
                s = (z_to - z + 4 + NZ) % NZ
                for yl_to in (0, 1):
                    for yh_to in (0, 1):
                        ht[tower, s // 8, yh_to * 2 + yl_to, s % 8, :, columns] = turned[
                            yl_to, z_to, yh_to
                        ]

    def gathered(tower, h):
        g_in[tower, h, q] = g_out[tower, h, q]
        ga_half(tower, h).wait_recv()

    def product(tower, h, side):
        g = g_in[tower, h].reshape(8 * HALF, 128)
        rows = ht[tower, side, :, :, :, pl.ds(512 * h, 512)].reshape(512, 512)
        return jnp.dot(rows, g, preferred_element_type=F32)

    def weight_first(tower):
        gathered(tower, 0)
        for side in (FAR, NEAR):
            w_first[side] = product(tower, 0, side)

    def weight(tower, side):
        term = (w_first[side] + product(tower, 1, side)).astype(BF16)
        y_out[tower, side] = term.reshape(4, 8, 16, 128)
        for o in (2, 1, 3):
            yb_copy(tower, side, o).start()

    def over_y(tower, side):
        yb_side(tower, side).wait_recv()
        total = y_out[tower, side, y].astype(F32)
        for o in (1, 2, 3):
            total = total + y_in[tower, side, o].astype(F32)
        z_out[tower, pl.ds(8 * side, 8)] = total.astype(BF16)

    def send_z(tower, side):
        for o in (FAR_OFFSETS if side == FAR else NEAR_OFFSETS):
            zc_copy(tower, o).start()

    def over_z(tower):
        z_in[tower, 0] = z_out[tower, 4]
        zc_all(tower).wait_recv()
        f_all[tower, grp] = jnp.sum(z_in[tower].astype(F32), axis=0).astype(BF16)
        for dy, dx, dc in ALL_GRP:
            fd_copy(tower, dy, dx, dc).start()

    def relays(tower):
        hid_all(tower).wait_recv()
        for o in (1, 2, 3):
            relay(tower, o).start()

    def clip_raw(h):
        if h == 0:
            share_grad.wait_recv()
        rows = pl.ds(HALF * h, HALF)
        raw_grad(CLIP, h, cacc[rows] + share_in[rows].astype(F32))

    def text_raw(h):
        rows = pl.ds(HALF * h, HALF)
        sums = back_in[0, 0, rows].astype(F32) + back_in[1, 0, rows].astype(F32)
        raw_grad(TEXT, h, part[0, rows] + sums)

    pieces = {
        0: lambda: (relays(CLIP), relays(TEXT)),
        2: lambda: (relay_all(CLIP).wait_recv(), turn(CLIP, 0, 0)),
        3: lambda: turn(CLIP, 0, 1),
        4: lambda: turn(CLIP, 0, 2),
        5: lambda: turn(CLIP, 0, 3),
        6: lambda: clip_raw(0),
        7: lambda: clip_raw(1),
        8: lambda: hidden_grad(CLIP),
        9: lambda: turn(CLIP, 1, 0),
        10: lambda: turn(CLIP, 1, 1),
        11: lambda: turn(CLIP, 1, 2),
        12: lambda: turn(CLIP, 1, 3),
        13: lambda: weight_first(CLIP),
        14: lambda: (gathered(CLIP, 1), weight(CLIP, FAR)),
        15: lambda: weight(CLIP, NEAR),
        16: lambda: (relay_all(TEXT).wait_recv(), turn(TEXT, 0, 0)),
        17: lambda: turn(TEXT, 0, 1),
        18: lambda: turn(TEXT, 0, 2),
        19: lambda: turn(TEXT, 0, 3),
        20: lambda: turn(TEXT, 1, 0),
        21: lambda: turn(TEXT, 1, 1),
        22: lambda: turn(TEXT, 1, 2),
        23: lambda: turn(TEXT, 1, 3),
        24: lambda: (over_y(CLIP, FAR), over_y(CLIP, NEAR)),
        25: lambda: ring_all(0, ring_s).wait_send(),
        26: lambda: ring_all(1, ring_s).wait_send(),
    }
    for j in range(6, -1, -1):
        for i in range(4):
            for d in (0, 1):
                if i >= 2:
                    send_sum(d, j + 1, LATE[d][i - 2])
                elif j >= 1:
                    send_sum(d, j, AHEAD[d][i])
                else:
                    back(d, 1, AHEAD[d][i]).wait_recv()
            pieces.get((6 - j) * 4 + i, lambda: None)()
    for i in (0, 1):
        for d in (0, 1):
            back(d, 1, LATE[d][i]).wait_recv()
        text_raw(i)
    send_z(CLIP, FAR)
    send_z(CLIP, NEAR)
    hidden_grad(TEXT)
    weight_first(TEXT)
    gathered(TEXT, 1)
    for side in (FAR, NEAR):
        weight(TEXT, side)
    for side in (FAR, NEAR):
        over_y(TEXT, side)
        send_z(TEXT, side)
    over_z(CLIP)
    for d in (0, 1):
        ring_all(d, back_s).wait_send()
    share_emb.wait_send()
    share_grad.wait_send()
    for tower in (CLIP, TEXT):
        hid_all(tower).wait_send()
        relay_all(tower).wait_send()
        ga_both(tower).wait_send()
        yb_both(tower).wait_send()
    zc_all(CLIP).wait_send()
    over_z(TEXT)
    zc_all(TEXT).wait_send()
    fd_all(CLIP).wait()
    fd_all(TEXT).wait()


def hand_over(clip_in, text_in, pieces, clip_hid, text_hid, clip_wg, text_wg, placed, sem):
    copies = [
        pltpu.make_async_copy(clip_in, clip_hid, sem.at[0]),
        pltpu.make_async_copy(text_in, text_hid, sem.at[1]),
        pltpu.make_async_copy(placed.at[CLIP], clip_wg, sem.at[2]),
        pltpu.make_async_copy(placed.at[TEXT], text_wg, sem.at[3]),
    ]
    copies[0].start()
    copies[1].start()
    for tower in (CLIP, TEXT):
        for j in range(16):
            rows, columns = pl.ds(16 * (j // 8), 16), pl.ds(128 * (j % 8), 128)
            placed[tower, rows, columns] = pieces[tower, j].astype(F32)
        copies[2 + tower].start()
    for copy in copies:
        copy.wait()


def local(hv, hc, wv, wc, match, multiplier, offset):
    vmem = pl.BlockSpec(memory_space=pltpu.VMEM)
    anywhere = pl.BlockSpec(memory_space=pl.ANY)
    dma = pltpu.SemaphoreType.DMA
    hidden = jax.ShapeDtypeStruct((TOK, D), BF16)
    gradient = jax.ShapeDtypeStruct((32, E), F32)
    results = pl.pallas_call(
        kernel,
        out_shape=(
            pltpu.VMEM((TOK, D), BF16),
            pltpu.VMEM((TOK, D), BF16),
            pltpu.VMEM((2, 16, 16, 128), BF16),
        ),
        in_specs=[pl.BlockSpec(memory_space=pltpu.HBM)] * 7,
        out_specs=(vmem,) * 3,
        scratch_shapes=[
            pltpu.VMEM((2, D, E), BF16),
            pltpu.VMEM((2, 8, TOK, D), BF16),
            pltpu.VMEM((2, 2, 4, 8, 16, 8 * TOK), BF16),
            pltpu.VMEM((2, TOK, E), F32),
            pltpu.VMEM((2, TOK, 1), F32),
            pltpu.VMEM((9, 2 * TOK, E), BF16),
            pltpu.VMEM((2 * TOK, E), BF16),
            pltpu.VMEM((9, 2 * TOK, E), F32),
            pltpu.VMEM((2 * TOK, E), F32),
            pltpu.VMEM((2, 8, TOK, E), BF16),
            pltpu.VMEM((2, 8, TOK, E), BF16),
            pltpu.VMEM((TOK, E), BF16),
            pltpu.VMEM((TOK, E), BF16),
            pltpu.VMEM((2, TOK, E), BF16),
            pltpu.VMEM((2, 2, 8, HALF, 128), BF16),
            pltpu.VMEM((2, 2, 8, HALF, 128), BF16),
            pltpu.VMEM((2, D // 2, 128), F32),
            pltpu.VMEM((2, 2, 4, 8, 16, 128), BF16),
            pltpu.VMEM((2, 2, 4, 8, 16, 128), BF16),
            pltpu.VMEM((2, NZ, 16, 128), BF16),
            pltpu.VMEM((2, NZ, 16, 128), BF16),
            pltpu.VMEM((32, TOK), jnp.int32),
            pltpu.SMEM((1,), F32),
            pltpu.SMEM((1,), F32),
            dma((7,)),
            dma((2,)),
            dma((2, 8, NC)),
            dma((2,)),
            dma((2, 8, NC)),
            dma((2,)),
            dma((2,)),
            dma((2,)),
            dma((2,)),
            dma((2,)),
            dma((2,)),
            dma((2,)),
            dma((2, 2)),
            dma((2,)),
            dma((2, 2)),
            dma((2,)),
            dma((2,)),
            dma((2,)),
            dma((2,)),
        ],
        compiler_params=pltpu.CompilerParams(
            collective_id=0, has_side_effects=True, vmem_limit_bytes=56 << 20
        ),
    )(hv, hc, wv, wc, match.reshape(32, TOK), multiplier, offset)
    return pl.pallas_call(
        hand_over,
        out_shape=(hidden, hidden, gradient, gradient),
        in_specs=[vmem] * 3,
        out_specs=(anywhere,) * 4,
        scratch_shapes=[pltpu.VMEM((2, 32, E), F32), dma((4,))],
    )(*(pltpu.with_memory_space_constraint(a, pltpu.VMEM) for a in results))


def solution(mesh):
    placed = (P(("grp", "blk"), None), P(("grp", "blk"), None), P(), P(), P("grp"), P(), P())
    return jax.shard_map(
        local,
        mesh=mesh,
        in_specs=placed,
        out_specs=(
            P(("grp", "blk"), None),
            P(("grp", "blk"), None),
            P("blk", None),
            P("blk", None),
        ),
        check_vma=False,
    )
```

```python
import jax
import jax.numpy as jnp
from jax import lax
from jax.experimental import pallas as pl
from jax.experimental.pallas import tpu as pltpu
from jax.sharding import PartitionSpec as P

MESH = pl.DeviceIdType.MESH
F32 = jnp.float32
BF16 = jnp.bfloat16
NX, NZ, TOK, D, E = 4, 16, 128, 1024, 1024
NC = 4
ROWS = TOK // NC
HALF = TOK // 2
LATE = ((0, 2), (1, 3))
AHEAD = ((1, 3), (0, 2))
COLUMNS = ((2, 1), (2, 0), (1, 1), (3, 1), (1, 0), (3, 0), (0, 1))
ALL_GRP = tuple((1,) + p for p in COLUMNS) + ((1, 0, 0),) + tuple((0,) + p for p in COLUMNS)
CLIP, TEXT = 0, 1
NEAR, FAR = 0, 1
FAR_OFFSETS = (8, 7, 9, 6, 10, 5, 11, 4)
NEAR_OFFSETS = (12, 3, 13, 2, 14, 1, 15)


def kernel(
    hv_hbm,
    hc_hbm,
    wv_hbm,
    wc_hbm,
    match_hbm,
    scale_hbm,
    shift_hbm,
    clip_hid,
    text_hid,
    f_all,
    w,
    hx,
    ht,
    unit,
    inverse,
    tt,
    emb,
    part,
    cacc,
    back_in,
    back_out,
    share_out,
    share_in,
    raw_out,
    g_out,
    g_in,
    w_first,
    y_out,
    y_in,
    z_out,
    z_in,
    match_ref,
    scale_ref,
    shift_ref,
    load_sem,
    ring_s,
    ring_r,
    back_s,
    back_r,
    share_s,
    share_r,
    hid_s,
    hid_r,
    rel_s,
    rel_r,
    ga_s,
    ga_r,
    yb_s,
    yb_r,
    zc_s,
    zc_r,
    fd_s,
    fd_r,
):
    grp = lax.axis_index("grp")
    blk = lax.axis_index("blk")
    yh, x, core = grp // 8, (grp // 2) % 4, grp % 2
    yl, z = blk // NZ, blk % NZ
    y = yh * 2 + yl
    q = x * 2 + core

    def place(x=x, y=y, z=z, core=core):
        return ((y // 2) * 8 + x * 2 + core, (y % 2) * NZ + z)

    right, left = place(z=(z + 1) % NZ), place(z=(z + NZ - 1) % NZ)
    partner = place(y=yh * 2 + 1 - yl)
    sibling = place(core=1 - core)

    def remote(src, dst, s, r, device):
        return pltpu.make_async_remote_copy(
            src_ref=src, dst_ref=dst, send_sem=s, recv_sem=r, device_id=device, device_id_type=MESH
        )

    loads = [
        pltpu.make_async_copy(hc_hbm, hx.at[TEXT, q], load_sem.at[0]),
        pltpu.make_async_copy(wc_hbm, w.at[TEXT], load_sem.at[1]),
        pltpu.make_async_copy(wv_hbm, w.at[CLIP], load_sem.at[2]),
        pltpu.make_async_copy(hv_hbm, hx.at[CLIP, q], load_sem.at[3]),
        pltpu.make_async_copy(match_hbm, match_ref, load_sem.at[4]),
        pltpu.make_async_copy(scale_hbm, scale_ref, load_sem.at[5]),
        pltpu.make_async_copy(shift_hbm, shift_ref, load_sem.at[6]),
    ]

    barrier = pltpu.get_barrier_semaphore()
    near = [right, left, sibling]
    near += [place(x=(x + o) % 4) for o in (1, 2, 3)] + [place(y=(y + o) % 4) for o in (1, 2, 3)]
    for device in near:
        pl.semaphore_signal(barrier, 1, device_id=device, device_id_type=MESH)
    loads[0].start()
    loads[1].start()

    def project(tower):
        raw = jnp.dot(hx[tower, q], w[tower], preferred_element_type=F32)
        size = jnp.sqrt(jnp.sum(raw * raw, axis=1, keepdims=True) + 1e-06)
        vec = raw * (1.0 / size)
        unit[tower] = vec
        inverse[tower] = 1.0 / size
        return vec.astype(BF16)

    def ring(d, k, c):
        first = isinstance(k, int) and k == 1
        last = isinstance(k, int) and k == 8
        src = tt.at[k - 1, pl.ds((0 if first else TOK * d) + ROWS * c, ROWS)]
        if first and c in AHEAD[d]:
            src = hx.at[TEXT, q, pl.ds(ROWS * c, ROWS)]
        dst = tt.at[k, pl.ds((0 if last else TOK * d) + ROWS * c, ROWS)]
        return remote(src, dst, ring_s.at[d], ring_r.at[d, k - 1, c], (right, left)[d])

    def back(d, k, c):
        rows = pl.ds(ROWS * c, ROWS)
        return remote(
            back_out.at[d, k - 1, rows],
            back_in.at[d, k - 1, rows],
            back_s.at[d],
            back_r.at[d, k - 1, c],
            (left, right)[d],
        )

    def hid_copy(tower, o):
        return remote(
            hx.at[tower, q],
            hx.at[tower, q],
            hid_s.at[tower],
            hid_r.at[tower],
            place(x=(x + o) % NX),
        )

    def relay(tower, o):
        index = ((x - o + 4) % 4) * 2 + core
        return remote(
            hx.at[tower, index], hx.at[tower, index], rel_s.at[tower], rel_r.at[tower], sibling
        )

    def ring_all(d, sems):
        chunks = tt.at[pl.ds(0, 5), pl.ds(0, 192)]
        return remote(chunks, chunks, sems.at[d], ring_r.at[d, 0, 0], right)

    def hid_all(tower):
        blocks = hx.at[tower, pl.ds(0, 3)]
        return remote(blocks, blocks, hid_s.at[tower], hid_r.at[tower], right)

    def relay_all(tower):
        blocks = hx.at[tower, pl.ds(0, 4)]
        return remote(blocks, blocks, rel_s.at[tower], rel_r.at[tower], sibling)

    loads[0].wait()
    pl.semaphore_wait(barrier, len(near))
    for i in (0, 1):
        for d in (0, 1):
            ring(d, 1, AHEAD[d][i]).start()
    loads[1].wait()
    for copy in loads[2:]:
        copy.start()
    tt[0, pl.ds(0, TOK)] = project(TEXT)
    for i in (0, 1):
        for d in (0, 1):
            ring(d, 1, LATE[d][i]).start()

    def forward(k, chunks):
        for i in (0, 1):
            for d in (0, 1):
                c = chunks[d][i]
                ring(d, k, c).wait_recv()
                if not (isinstance(k, int) and k == 7 and c in AHEAD[d]):
                    ring(d, k + 1, c).start()

    forward(1, AHEAD)
    loads[2].wait()
    loads[3].wait()
    emb[pl.ds(0, TOK)] = project(CLIP)
    share_emb = remote(
        emb.at[pl.ds(0, TOK)], emb.at[pl.ds(TOK, TOK)], share_s.at[0], share_r.at[0], partner
    )
    share_emb.start()
    for tower in (CLIP, TEXT):
        for o in (1, 3, 2):
            hid_copy(tower, o).start()
        relay(tower, 0).start()

    for copy in loads[4:]:
        copy.wait()
    scale = scale_ref[0]
    shift = shift_ref[0]

    def embeddings(k):
        chunks = [tt[k, pl.ds(ROWS * c, ROWS)] for c in range(2 * NC)]
        hidden = [c for c in range(2 * NC) if c % NC in AHEAD[c // NC]]
        raw = jnp.dot(
            jnp.concatenate([chunks[c] for c in hidden], axis=0),
            w[TEXT],
            preferred_element_type=F32,
        )
        size = jnp.sqrt(jnp.sum(raw * raw, axis=1, keepdims=True) + 1e-06)
        vec = (raw * (1.0 / size)).astype(BF16)
        for i, c in enumerate(hidden):
            chunks[c] = vec[ROWS * i : ROWS * (i + 1)]
        return jnp.concatenate(chunks, axis=0)

    def work(k, rows):
        base0 = (yl * NZ + (z - k + NZ) % NZ) * TOK
        base1 = (yl * NZ + (z + k) % NZ) * TOK
        t = embeddings(k) if rows == 2 * TOK else tt[k, pl.ds(0, rows)]
        a = emb[...]
        scores = scale * lax.dot_general(
            t, a, (((1,), (1,)), ((), ())), preferred_element_type=F32
        ) + shift
        row = lax.broadcasted_iota(jnp.int32, (rows, 2 * TOK), 0)
        place_of = jnp.where(row < TOK, base0 + row, base1 + row - TOK)
        wanted = jnp.concatenate(
            [match_ref[pl.ds(blk, 1), :], match_ref[pl.ds((1 - yl) * NZ + z, 1), :]], axis=1
        )
        hit = place_of == wanted
        flipped = jnp.where(hit, scores, -scores)
        coef = (jnp.where(hit, -scale, scale) / (1.0 + jnp.exp(flipped))).astype(BF16)
        part[k, pl.ds(0, rows)] = jnp.dot(coef, a, preferred_element_type=F32)
        return lax.dot_general(coef, t, (((0,), (0,)), ((), ())), preferred_element_type=F32)

    forward(1, LATE)
    share_emb.wait_recv()
    cacc[...] = work(0, TOK)

    @pl.loop(2, 7)
    def _(k):
        forward(k, AHEAD)
        cacc[...] += work(k - 1, 2 * TOK)
        forward(k, LATE)

    def run(d, k, c):
        return part[k, pl.ds((0 if k == 8 else TOK * d) + ROWS * c, ROWS)]

    def send_fresh(d, k, c):
        back_out[d, k - 1, pl.ds(ROWS * c, ROWS)] = run(d, k, c).astype(BF16)
        back(d, k, c).start()

    def send_sum(d, k, c):
        rows = pl.ds(ROWS * c, ROWS)
        back(d, k + 1, c).wait_recv()
        back_out[d, k - 1, rows] = (run(d, k, c) + back_in[d, k, rows].astype(F32)).astype(BF16)
        back(d, k, c).start()

    forward(7, AHEAD)
    cacc[...] += work(6, 2 * TOK)
    forward(7, LATE)
    cacc[...] += work(7, 2 * TOK)

    for i in (0, 1):
        for d in (0, 1):
            send_fresh(d, 7, AHEAD[d][i])
    for i in (0, 1):
        for d in (0, 1):
            ring(d, 8, LATE[d][i]).wait_recv()
    cacc[...] += work(8, TOK)
    for i in (0, 1):
        for d in (0, 1):
            send_fresh(d, 8, LATE[d][i])

    share_out[...] = cacc[pl.ds(TOK, TOK)].astype(BF16)
    share_grad = remote(share_out, share_in, share_s.at[1], share_r.at[1], partner)
    share_grad.start()

    def ga_copy(tower, h, dx, dc):
        to = ((x + dx) % 4) * 2 + (core + dc) % 2
        return remote(
            g_out.at[tower, h, to],
            g_in.at[tower, h, q],
            ga_s.at[tower],
            ga_r.at[tower, h],
            place(x=(x + dx) % 4, core=(core + dc) % 2),
        )

    def yb_copy(tower, side, o):
        to = (y + o) % 4
        return remote(
            y_out.at[tower, side, to],
            y_in.at[tower, side, o],
            yb_s.at[tower],
            yb_r.at[tower, side],
            place(y=to),
        )

    def ga_half(tower, h):
        parts = g_in.at[tower, h, pl.ds(0, 7)]
        return remote(parts, parts, ga_s.at[tower], ga_r.at[tower, h], sibling)

    def ga_both(tower):
        parts = g_out.at[tower, :, pl.ds(0, 7)]
        return remote(parts, parts, ga_s.at[tower], ga_r.at[tower, 0], sibling)

    def yb_side(tower, side):
        parts = y_in.at[tower, side, pl.ds(1, 3)]
        return remote(parts, parts, yb_s.at[tower], yb_r.at[tower, side], partner)

    def yb_both(tower):
        parts = y_out.at[tower, :, pl.ds(0, 3)]
        return remote(parts, parts, yb_s.at[tower], yb_r.at[tower, 0], partner)

    def zc_copy(tower, o):
        to = (z + o) % NZ
        return remote(
            z_out.at[tower, (o + 4) % NZ], z_in.at[tower, o], zc_s.at[tower], zc_r.at[tower], place(z=to)
        )

    def zc_all(tower):
        rest = pl.ds(1, NZ - 1)
        return remote(
            z_out.at[tower, rest], z_in.at[tower, rest], zc_s.at[tower], zc_r.at[tower], right
        )

    def fd_copy(tower, dy, dx, dc):
        to = ((yh + dy) % 2) * 8 + ((x + dx) % 4) * 2 + (core + dc) % 2
        return remote(
            f_all.at[tower, grp], f_all.at[tower, grp], fd_s.at[tower], fd_r.at[tower], (to, blk)
        )

    def fd_all(tower):
        rest = f_all.at[tower, pl.ds(0, 15)]
        return remote(rest, rest, fd_s.at[tower], fd_r.at[tower], right)

    def raw_grad(tower, h, grad):
        rows = pl.ds(HALF * h, HALF)
        vec = unit[tower, rows]
        radial = jnp.sum(vec * grad, axis=1, keepdims=True)
        raw = ((grad - vec * radial) * inverse[tower, rows]).astype(BF16)
        for j in range(8):
            g_out[tower, h, j] = raw[:, 128 * j : 128 * (j + 1)]
        for dx, dc in COLUMNS:
            ga_copy(tower, h, dx, dc).start()
        raw_out[tower, rows] = raw

    def hidden_grad(tower):
        (clip_hid, text_hid)[tower][...] = lax.dot_general(
            raw_out[tower], w[tower], (((1,), (1,)), ((), ())), preferred_element_type=F32
        ).astype(BF16)

    def turn(tower, h, *pairs):
        rows = pl.ds(HALF * h, HALF)
        for j in pairs:
            two = jnp.concatenate([hx[tower, 2 * j, rows], hx[tower, 2 * j + 1, rows]], axis=0)
            turned = two.T.reshape(2, NZ, 2, 16, 128)
            columns = pl.ds(512 * h + 128 * j, 128)
            for z_to in range(NZ):
                s = (z_to - z + 4 + NZ) % NZ
                for yl_to in (0, 1):
                    for yh_to in (0, 1):
                        ht[tower, s // 8, yh_to * 2 + yl_to, s % 8, :, columns] = turned[
                            yl_to, z_to, yh_to
                        ]

    def gathered(tower, h):
        g_in[tower, h, q] = g_out[tower, h, q]
        ga_half(tower, h).wait_recv()

    def product(tower, h, side):
        g = g_in[tower, h].reshape(8 * HALF, 128)
        rows = ht[tower, side, :, :, :, pl.ds(512 * h, 512)].reshape(512, 512)
        return jnp.dot(rows, g, preferred_element_type=F32)

    def weight_first(tower):
        gathered(tower, 0)
        for side in (FAR, NEAR):
            w_first[side] = product(tower, 0, side)

    def weight(tower, side):
        term = (w_first[side] + product(tower, 1, side)).astype(BF16)
        y_out[tower, side] = term.reshape(4, 8, 16, 128)
        for o in (2, 1, 3):
            yb_copy(tower, side, o).start()

    def over_y(tower, side):
        yb_side(tower, side).wait_recv()
        total = y_out[tower, side, y].astype(F32)
        for o in (1, 2, 3):
            total = total + y_in[tower, side, o].astype(F32)
        z_out[tower, pl.ds(8 * side, 8)] = total.astype(BF16)

    def send_z(tower, side):
        for o in (FAR_OFFSETS if side == FAR else NEAR_OFFSETS):
            zc_copy(tower, o).start()

    def over_z(tower):
        z_in[tower, 0] = z_out[tower, 4]
        zc_all(tower).wait_recv()
        f_all[tower, grp] = jnp.sum(z_in[tower].astype(F32), axis=0).astype(BF16)
        for dy, dx, dc in ALL_GRP:
            fd_copy(tower, dy, dx, dc).start()

    def relays(tower):
        hid_all(tower).wait_recv()
        for o in (1, 2, 3):
            relay(tower, o).start()

    def clip_raw(h):
        if h == 0:
            share_grad.wait_recv()
        rows = pl.ds(HALF * h, HALF)
        raw_grad(CLIP, h, cacc[rows] + share_in[rows].astype(F32))

    def text_raw(h):
        rows = pl.ds(HALF * h, HALF)
        sums = back_in[0, 0, rows].astype(F32) + back_in[1, 0, rows].astype(F32)
        raw_grad(TEXT, h, part[0, rows] + sums)

    pieces = {
        0: lambda: (relays(CLIP), relays(TEXT)),
        2: lambda: (relay_all(CLIP).wait_recv(), turn(CLIP, 0, 0)),
        3: lambda: turn(CLIP, 0, 1),
        4: lambda: turn(CLIP, 0, 2),
        5: lambda: turn(CLIP, 0, 3),
        6: lambda: clip_raw(0),
        7: lambda: clip_raw(1),
        8: lambda: hidden_grad(CLIP),
        9: lambda: turn(CLIP, 1, 0),
        10: lambda: turn(CLIP, 1, 1),
        11: lambda: turn(CLIP, 1, 2),
        12: lambda: turn(CLIP, 1, 3),
        13: lambda: weight_first(CLIP),
        14: lambda: (gathered(CLIP, 1), weight(CLIP, FAR)),
        15: lambda: weight(CLIP, NEAR),
        16: lambda: (relay_all(TEXT).wait_recv(), turn(TEXT, 0, 0)),
        17: lambda: turn(TEXT, 0, 1),
        18: lambda: turn(TEXT, 0, 2),
        19: lambda: turn(TEXT, 0, 3),
        20: lambda: turn(TEXT, 1, 0),
        21: lambda: turn(TEXT, 1, 1),
        22: lambda: turn(TEXT, 1, 2),
        23: lambda: turn(TEXT, 1, 3),
        24: lambda: (over_y(CLIP, FAR), over_y(CLIP, NEAR)),
        25: lambda: ring_all(0, ring_s).wait_send(),
        26: lambda: ring_all(1, ring_s).wait_send(),
    }
    for j in range(6, -1, -1):
        for i in range(4):
            for d in (0, 1):
                if i >= 2:
                    send_sum(d, j + 1, LATE[d][i - 2])
                elif j >= 1:
                    send_sum(d, j, AHEAD[d][i])
                else:
                    back(d, 1, AHEAD[d][i]).wait_recv()
            pieces.get((6 - j) * 4 + i, lambda: None)()
    for i in (0, 1):
        for d in (0, 1):
            back(d, 1, LATE[d][i]).wait_recv()
        text_raw(i)
    send_z(CLIP, FAR)
    send_z(CLIP, NEAR)
    weight_first(TEXT)
    gathered(TEXT, 1)
    for side in (FAR, NEAR):
        weight(TEXT, side)
    for side in (FAR, NEAR):
        over_y(TEXT, side)
        send_z(TEXT, side)
    hidden_grad(TEXT)
    over_z(CLIP)
    for d in (0, 1):
        ring_all(d, back_s).wait_send()
    share_emb.wait_send()
    share_grad.wait_send()
    for tower in (CLIP, TEXT):
        hid_all(tower).wait_send()
        relay_all(tower).wait_send()
        ga_both(tower).wait_send()
        yb_both(tower).wait_send()
    zc_all(CLIP).wait_send()
    over_z(TEXT)
    zc_all(TEXT).wait_send()
    fd_all(CLIP).wait()
    fd_all(TEXT).wait()


def hand_over(clip_in, text_in, pieces, clip_hid, text_hid, clip_wg, text_wg, placed, sem):
    copies = [
        pltpu.make_async_copy(clip_in, clip_hid, sem.at[0]),
        pltpu.make_async_copy(text_in, text_hid, sem.at[1]),
        pltpu.make_async_copy(placed.at[CLIP], clip_wg, sem.at[2]),
        pltpu.make_async_copy(placed.at[TEXT], text_wg, sem.at[3]),
    ]
    copies[0].start()
    copies[1].start()
    for tower in (CLIP, TEXT):
        for j in range(16):
            rows, columns = pl.ds(16 * (j // 8), 16), pl.ds(128 * (j % 8), 128)
            placed[tower, rows, columns] = pieces[tower, j].astype(F32)
        copies[2 + tower].start()
    for copy in copies:
        copy.wait()


def local(hv, hc, wv, wc, match, multiplier, offset):
    vmem = pl.BlockSpec(memory_space=pltpu.VMEM)
    anywhere = pl.BlockSpec(memory_space=pl.ANY)
    dma = pltpu.SemaphoreType.DMA
    hidden = jax.ShapeDtypeStruct((TOK, D), BF16)
    gradient = jax.ShapeDtypeStruct((32, E), F32)
    results = pl.pallas_call(
        kernel,
        out_shape=(
            pltpu.VMEM((TOK, D), BF16),
            pltpu.VMEM((TOK, D), BF16),
            pltpu.VMEM((2, 16, 16, 128), BF16),
        ),
        in_specs=[pl.BlockSpec(memory_space=pltpu.HBM)] * 7,
        out_specs=(vmem,) * 3,
        scratch_shapes=[
            pltpu.VMEM((2, D, E), BF16),
            pltpu.VMEM((2, 8, TOK, D), BF16),
            pltpu.VMEM((2, 2, 4, 8, 16, 8 * TOK), BF16),
            pltpu.VMEM((2, TOK, E), F32),
            pltpu.VMEM((2, TOK, 1), F32),
            pltpu.VMEM((9, 2 * TOK, E), BF16),
            pltpu.VMEM((2 * TOK, E), BF16),
            pltpu.VMEM((9, 2 * TOK, E), F32),
            pltpu.VMEM((2 * TOK, E), F32),
            pltpu.VMEM((2, 8, TOK, E), BF16),
            pltpu.VMEM((2, 8, TOK, E), BF16),
            pltpu.VMEM((TOK, E), BF16),
            pltpu.VMEM((TOK, E), BF16),
            pltpu.VMEM((2, TOK, E), BF16),
            pltpu.VMEM((2, 2, 8, HALF, 128), BF16),
            pltpu.VMEM((2, 2, 8, HALF, 128), BF16),
            pltpu.VMEM((2, D // 2, 128), F32),
            pltpu.VMEM((2, 2, 4, 8, 16, 128), BF16),
            pltpu.VMEM((2, 2, 4, 8, 16, 128), BF16),
            pltpu.VMEM((2, NZ, 16, 128), BF16),
            pltpu.VMEM((2, NZ, 16, 128), BF16),
            pltpu.VMEM((32, TOK), jnp.int32),
            pltpu.SMEM((1,), F32),
            pltpu.SMEM((1,), F32),
            dma((7,)),
            dma((2,)),
            dma((2, 8, NC)),
            dma((2,)),
            dma((2, 8, NC)),
            dma((2,)),
            dma((2,)),
            dma((2,)),
            dma((2,)),
            dma((2,)),
            dma((2,)),
            dma((2,)),
            dma((2, 2)),
            dma((2,)),
            dma((2, 2)),
            dma((2,)),
            dma((2,)),
            dma((2,)),
            dma((2,)),
        ],
        compiler_params=pltpu.CompilerParams(
            collective_id=0, has_side_effects=True, vmem_limit_bytes=56 << 20
        ),
    )(hv, hc, wv, wc, match.reshape(32, TOK), multiplier, offset)
    return pl.pallas_call(
        hand_over,
        out_shape=(hidden, hidden, gradient, gradient),
        in_specs=[vmem] * 3,
        out_specs=(anywhere,) * 4,
        scratch_shapes=[pltpu.VMEM((2, 32, E), F32), dma((4,))],
    )(*(pltpu.with_memory_space_constraint(a, pltpu.VMEM) for a in results))


def solution(mesh):
    placed = (P(("grp", "blk"), None), P(("grp", "blk"), None), P(), P(), P("grp"), P(), P())
    return jax.shard_map(
        local,
        mesh=mesh,
        in_specs=placed,
        out_specs=(
            P(("grp", "blk"), None),
            P(("grp", "blk"), None),
            P("blk", None),
            P("blk", None),
        ),
        check_vma=False,
    )
```

```python
import jax
import jax.numpy as jnp
from jax import lax
from jax.experimental import pallas as pl
from jax.experimental.pallas import tpu as pltpu
from jax.sharding import PartitionSpec as P

MESH = pl.DeviceIdType.MESH
F32 = jnp.float32
BF16 = jnp.bfloat16
NX, NZ, TOK, D, E = 4, 16, 128, 1024, 1024
NC = 4
ROWS = TOK // NC
HALF = TOK // 2
LATE = ((0, 2), (1, 3))
AHEAD = ((1, 3), (0, 2))
COLUMNS = ((2, 1), (2, 0), (1, 1), (3, 1), (1, 0), (3, 0), (0, 1))
ALL_GRP = tuple((1,) + p for p in COLUMNS) + ((1, 0, 0),) + tuple((0,) + p for p in COLUMNS)
CLIP, TEXT = 0, 1
NEAR, FAR = 0, 1
FAR_OFFSETS = (8, 7, 9, 6, 10, 5, 11, 4)
NEAR_OFFSETS = (12, 3, 13, 2, 14, 1, 15)


def kernel(
    hv_hbm,
    hc_hbm,
    wv_hbm,
    wc_hbm,
    match_hbm,
    scale_hbm,
    shift_hbm,
    clip_hid,
    text_hid,
    f_all,
    w,
    hx,
    ht,
    unit,
    inverse,
    tt,
    emb,
    part,
    cacc,
    back_in,
    back_out,
    share_out,
    share_in,
    raw_out,
    g_out,
    g_in,
    w_first,
    y_out,
    y_in,
    z_out,
    z_in,
    match_ref,
    scale_ref,
    shift_ref,
    load_sem,
    ring_s,
    ring_r,
    back_s,
    back_r,
    share_s,
    share_r,
    hid_s,
    hid_r,
    rel_s,
    rel_r,
    ga_s,
    ga_r,
    yb_s,
    yb_r,
    zc_s,
    zc_r,
    fd_s,
    fd_r,
):
    grp = lax.axis_index("grp")
    blk = lax.axis_index("blk")
    yh, x, core = grp // 8, (grp // 2) % 4, grp % 2
    yl, z = blk // NZ, blk % NZ
    y = yh * 2 + yl
    q = x * 2 + core

    def place(x=x, y=y, z=z, core=core):
        return ((y // 2) * 8 + x * 2 + core, (y % 2) * NZ + z)

    right, left = place(z=(z + 1) % NZ), place(z=(z + NZ - 1) % NZ)
    partner = place(y=yh * 2 + 1 - yl)
    sibling = place(core=1 - core)

    def remote(src, dst, s, r, device):
        return pltpu.make_async_remote_copy(
            src_ref=src, dst_ref=dst, send_sem=s, recv_sem=r, device_id=device, device_id_type=MESH
        )

    loads = [
        pltpu.make_async_copy(hc_hbm, hx.at[TEXT, q], load_sem.at[0]),
        pltpu.make_async_copy(wc_hbm, w.at[TEXT], load_sem.at[1]),
        pltpu.make_async_copy(wv_hbm, w.at[CLIP], load_sem.at[2]),
        pltpu.make_async_copy(hv_hbm, hx.at[CLIP, q], load_sem.at[3]),
        pltpu.make_async_copy(match_hbm, match_ref, load_sem.at[4]),
        pltpu.make_async_copy(scale_hbm, scale_ref, load_sem.at[5]),
        pltpu.make_async_copy(shift_hbm, shift_ref, load_sem.at[6]),
    ]

    barrier = pltpu.get_barrier_semaphore()
    near = [right, left, sibling]
    near += [place(x=(x + o) % 4) for o in (1, 2, 3)] + [place(y=(y + o) % 4) for o in (1, 2, 3)]
    for device in near:
        pl.semaphore_signal(barrier, 1, device_id=device, device_id_type=MESH)
    loads[0].start()
    loads[1].start()

    def project(tower):
        raw = jnp.dot(hx[tower, q], w[tower], preferred_element_type=F32)
        size = jnp.sqrt(jnp.sum(raw * raw, axis=1, keepdims=True) + 1e-06)
        vec = raw * (1.0 / size)
        unit[tower] = vec
        inverse[tower] = 1.0 / size
        return vec.astype(BF16)

    def ring(d, k, c):
        first = isinstance(k, int) and k == 1
        last = isinstance(k, int) and k == 8
        src = tt.at[k - 1, pl.ds((0 if first else TOK * d) + ROWS * c, ROWS)]
        if first and c in AHEAD[d]:
            src = hx.at[TEXT, q, pl.ds(ROWS * c, ROWS)]
        dst = tt.at[k, pl.ds((0 if last else TOK * d) + ROWS * c, ROWS)]
        return remote(src, dst, ring_s.at[d], ring_r.at[d, k - 1, c], (right, left)[d])

    def back(d, k, c):
        rows = pl.ds(ROWS * c, ROWS)
        return remote(
            back_out.at[d, k - 1, rows],
            back_in.at[d, k - 1, rows],
            back_s.at[d],
            ring_r.at[d, k - 1, c] if k <= 5 else back_r.at[d, k - 6, c],
            (left, right)[d],
        )

    def hid_copy(tower, o):
        return remote(
            hx.at[tower, q],
            hx.at[tower, q],
            hid_s.at[tower],
            hid_r.at[tower],
            place(x=(x + o) % NX),
        )

    def relay(tower, o):
        index = ((x - o + 4) % 4) * 2 + core
        return remote(
            hx.at[tower, index], hx.at[tower, index], rel_s.at[tower], rel_r.at[tower], sibling
        )

    def ring_all(d, sems):
        chunks = tt.at[pl.ds(0, 5), pl.ds(0, 192)]
        return remote(chunks, chunks, sems.at[d], ring_r.at[d, 0, 0], right)

    def hid_all(tower):
        blocks = hx.at[tower, pl.ds(0, 3)]
        return remote(blocks, blocks, hid_s.at[tower], hid_r.at[tower], right)

    def relay_all(tower):
        blocks = hx.at[tower, pl.ds(0, 4)]
        return remote(blocks, blocks, rel_s.at[tower], rel_r.at[tower], sibling)

    loads[0].wait()
    pl.semaphore_wait(barrier, len(near))
    for i in (0, 1):
        for d in (0, 1):
            ring(d, 1, AHEAD[d][i]).start()
    loads[1].wait()
    for copy in loads[2:]:
        copy.start()
    tt[0, pl.ds(0, TOK)] = project(TEXT)
    for i in (0, 1):
        for d in (0, 1):
            ring(d, 1, LATE[d][i]).start()

    def forward(k, chunks):
        for i in (0, 1):
            for d in (0, 1):
                c = chunks[d][i]
                ring(d, k, c).wait_recv()
                if not (isinstance(k, int) and k == 7 and c in AHEAD[d]):
                    ring(d, k + 1, c).start()

    forward(1, AHEAD)
    loads[2].wait()
    loads[3].wait()
    emb[pl.ds(0, TOK)] = project(CLIP)
    share_emb = remote(
        emb.at[pl.ds(0, TOK)], emb.at[pl.ds(TOK, TOK)], share_s.at[0], share_r.at[0], partner
    )
    share_emb.start()
    for tower in (CLIP, TEXT):
        for o in (1, 3, 2):
            hid_copy(tower, o).start()
        relay(tower, 0).start()

    for copy in loads[4:]:
        copy.wait()
    scale = scale_ref[0]
    shift = shift_ref[0]

    def embeddings(k):
        chunks = [tt[k, pl.ds(ROWS * c, ROWS)] for c in range(2 * NC)]
        hidden = [c for c in range(2 * NC) if c % NC in AHEAD[c // NC]]
        raw = jnp.dot(
            jnp.concatenate([chunks[c] for c in hidden], axis=0),
            w[TEXT],
            preferred_element_type=F32,
        )
        size = jnp.sqrt(jnp.sum(raw * raw, axis=1, keepdims=True) + 1e-06)
        vec = (raw * (1.0 / size)).astype(BF16)
        for i, c in enumerate(hidden):
            chunks[c] = vec[ROWS * i : ROWS * (i + 1)]
        return jnp.concatenate(chunks, axis=0)

    def work(k, rows):
        base0 = (yl * NZ + (z - k + NZ) % NZ) * TOK
        base1 = (yl * NZ + (z + k) % NZ) * TOK
        t = embeddings(k) if rows == 2 * TOK else tt[k, pl.ds(0, rows)]
        a = emb[...]
        scores = scale * lax.dot_general(
            t, a, (((1,), (1,)), ((), ())), preferred_element_type=F32
        ) + shift
        row = lax.broadcasted_iota(jnp.int32, (rows, 2 * TOK), 0)
        place_of = jnp.where(row < TOK, base0 + row, base1 + row - TOK)
        wanted = jnp.concatenate(
            [match_ref[pl.ds(blk, 1), :], match_ref[pl.ds((1 - yl) * NZ + z, 1), :]], axis=1
        )
        hit = place_of == wanted
        flipped = jnp.where(hit, scores, -scores)
        coef = (jnp.where(hit, -scale, scale) / (1.0 + jnp.exp(flipped))).astype(BF16)
        part[k, pl.ds(0, rows)] = jnp.dot(coef, a, preferred_element_type=F32)
        return lax.dot_general(coef, t, (((0,), (0,)), ((), ())), preferred_element_type=F32)

    forward(1, LATE)
    share_emb.wait_recv()
    cacc[...] = work(0, TOK)

    @pl.loop(2, 7)
    def _(k):
        forward(k, AHEAD)
        cacc[...] += work(k - 1, 2 * TOK)
        forward(k, LATE)

    def run(d, k, c):
        return part[k, pl.ds((0 if k == 8 else TOK * d) + ROWS * c, ROWS)]

    def send_fresh(d, k, c):
        back_out[d, k - 1, pl.ds(ROWS * c, ROWS)] = run(d, k, c).astype(BF16)
        back(d, k, c).start()

    def send_sum(d, k, c):
        rows = pl.ds(ROWS * c, ROWS)
        back(d, k + 1, c).wait_recv()
        back_out[d, k - 1, rows] = (run(d, k, c) + back_in[d, k, rows].astype(F32)).astype(BF16)
        back(d, k, c).start()

    forward(7, AHEAD)
    cacc[...] += work(6, 2 * TOK)
    forward(7, LATE)
    cacc[...] += work(7, 2 * TOK)

    for i in (0, 1):
        for d in (0, 1):
            send_fresh(d, 7, AHEAD[d][i])
    for i in (0, 1):
        for d in (0, 1):
            ring(d, 8, LATE[d][i]).wait_recv()
    cacc[...] += work(8, TOK)
    for i in (0, 1):
        for d in (0, 1):
            send_fresh(d, 8, LATE[d][i])

    share_out[...] = cacc[pl.ds(TOK, TOK)].astype(BF16)
    share_grad = remote(share_out, share_in, share_s.at[1], share_r.at[1], partner)
    share_grad.start()

    def ga_copy(tower, h, dx, dc):
        to = ((x + dx) % 4) * 2 + (core + dc) % 2
        return remote(
            g_out.at[tower, h, to],
            g_in.at[tower, h, q],
            ga_s.at[tower],
            ga_r.at[tower, h],
            place(x=(x + dx) % 4, core=(core + dc) % 2),
        )

    def yb_copy(tower, side, o):
        to = (y + o) % 4
        return remote(
            y_out.at[tower, side, to],
            y_in.at[tower, side, o],
            yb_s.at[tower],
            yb_r.at[tower, side],
            place(y=to),
        )

    def ga_half(tower, h):
        parts = g_in.at[tower, h, pl.ds(0, 7)]
        return remote(parts, parts, ga_s.at[tower], ga_r.at[tower, h], sibling)

    def ga_both(tower):
        parts = g_out.at[tower, :, pl.ds(0, 7)]
        return remote(parts, parts, ga_s.at[tower], ga_r.at[tower, 0], sibling)

    def yb_side(tower, side):
        parts = y_in.at[tower, side, pl.ds(1, 3)]
        return remote(parts, parts, yb_s.at[tower], yb_r.at[tower, side], partner)

    def yb_both(tower):
        parts = y_out.at[tower, :, pl.ds(0, 3)]
        return remote(parts, parts, yb_s.at[tower], yb_r.at[tower, 0], partner)

    def zc_copy(tower, o):
        to = (z + o) % NZ
        return remote(
            z_out.at[tower, (o + 4) % NZ], z_in.at[tower, o], zc_s.at[tower], zc_r.at[tower], place(z=to)
        )

    def zc_all(tower):
        rest = pl.ds(1, NZ - 1)
        return remote(
            z_out.at[tower, rest], z_in.at[tower, rest], zc_s.at[tower], zc_r.at[tower], right
        )

    def fd_copy(tower, dy, dx, dc):
        to = ((yh + dy) % 2) * 8 + ((x + dx) % 4) * 2 + (core + dc) % 2
        return remote(
            f_all.at[tower, grp], f_all.at[tower, grp], fd_s.at[tower], fd_r.at[tower], (to, blk)
        )

    def fd_all(tower):
        rest = f_all.at[tower, pl.ds(0, 15)]
        return remote(rest, rest, fd_s.at[tower], fd_r.at[tower], right)

    def raw_grad(tower, h, grad):
        rows = pl.ds(HALF * h, HALF)
        vec = unit[tower, rows]
        radial = jnp.sum(vec * grad, axis=1, keepdims=True)
        raw = ((grad - vec * radial) * inverse[tower, rows]).astype(BF16)
        for j in range(8):
            g_out[tower, h, j] = raw[:, 128 * j : 128 * (j + 1)]
        for dx, dc in COLUMNS:
            ga_copy(tower, h, dx, dc).start()
        raw_out[tower, rows] = raw

    def hidden_grad(tower):
        (clip_hid, text_hid)[tower][...] = lax.dot_general(
            raw_out[tower], w[tower], (((1,), (1,)), ((), ())), preferred_element_type=F32
        ).astype(BF16)

    def turn(tower, h, *pairs):
        rows = pl.ds(HALF * h, HALF)
        for j in pairs:
            two = jnp.concatenate([hx[tower, 2 * j, rows], hx[tower, 2 * j + 1, rows]], axis=0)
            turned = two.T.reshape(2, NZ, 2, 16, 128)
            columns = pl.ds(512 * h + 128 * j, 128)
            for z_to in range(NZ):
                s = (z_to - z + 4 + NZ) % NZ
                for yl_to in (0, 1):
                    for yh_to in (0, 1):
                        ht[tower, s // 8, yh_to * 2 + yl_to, s % 8, :, columns] = turned[
                            yl_to, z_to, yh_to
                        ]

    def gathered(tower, h):
        g_in[tower, h, q] = g_out[tower, h, q]
        ga_half(tower, h).wait_recv()

    def product(tower, h, side):
        g = g_in[tower, h].reshape(8 * HALF, 128)
        rows = ht[tower, side, :, :, :, pl.ds(512 * h, 512)].reshape(512, 512)
        return jnp.dot(rows, g, preferred_element_type=F32)

    def weight_first(tower):
        gathered(tower, 0)
        for side in (FAR, NEAR):
            w_first[side] = product(tower, 0, side)

    def weight(tower, side):
        term = (w_first[side] + product(tower, 1, side)).astype(BF16)
        y_out[tower, side] = term.reshape(4, 8, 16, 128)
        for o in (2, 1, 3):
            yb_copy(tower, side, o).start()

    def over_y(tower, side):
        yb_side(tower, side).wait_recv()
        total = y_out[tower, side, y].astype(F32)
        for o in (1, 2, 3):
            total = total + y_in[tower, side, o].astype(F32)
        z_out[tower, pl.ds(8 * side, 8)] = total.astype(BF16)

    def send_z(tower, side):
        for o in (FAR_OFFSETS if side == FAR else NEAR_OFFSETS):
            zc_copy(tower, o).start()

    def over_z(tower):
        z_in[tower, 0] = z_out[tower, 4]
        zc_all(tower).wait_recv()
        f_all[tower, grp] = jnp.sum(z_in[tower].astype(F32), axis=0).astype(BF16)
        for dy, dx, dc in ALL_GRP:
            fd_copy(tower, dy, dx, dc).start()

    def relays(tower):
        hid_all(tower).wait_recv()
        for o in (1, 2, 3):
            relay(tower, o).start()

    def clip_raw(h):
        if h == 0:
            share_grad.wait_recv()
        rows = pl.ds(HALF * h, HALF)
        raw_grad(CLIP, h, cacc[rows] + share_in[rows].astype(F32))

    def text_raw(h):
        rows = pl.ds(HALF * h, HALF)
        sums = back_in[0, 0, rows].astype(F32) + back_in[1, 0, rows].astype(F32)
        raw_grad(TEXT, h, part[0, rows] + sums)

    pieces = {
        0: lambda: (relays(CLIP), relays(TEXT)),
        2: lambda: (relay_all(CLIP).wait_recv(), turn(CLIP, 0, 0)),
        3: lambda: turn(CLIP, 0, 1),
        4: lambda: turn(CLIP, 0, 2),
        5: lambda: turn(CLIP, 0, 3),
        6: lambda: clip_raw(0),
        7: lambda: clip_raw(1),
        8: lambda: hidden_grad(CLIP),
        9: lambda: turn(CLIP, 1, 0),
        10: lambda: turn(CLIP, 1, 1),
        11: lambda: turn(CLIP, 1, 2),
        12: lambda: turn(CLIP, 1, 3),
        13: lambda: weight_first(CLIP),
        14: lambda: (gathered(CLIP, 1), weight(CLIP, FAR)),
        15: lambda: weight(CLIP, NEAR),
        16: lambda: (relay_all(TEXT).wait_recv(), turn(TEXT, 0, 0)),
        17: lambda: turn(TEXT, 0, 1),
        18: lambda: turn(TEXT, 0, 2),
        19: lambda: turn(TEXT, 0, 3),
        20: lambda: turn(TEXT, 1, 0),
        21: lambda: turn(TEXT, 1, 1),
        22: lambda: turn(TEXT, 1, 2),
        23: lambda: turn(TEXT, 1, 3),
        24: lambda: (over_y(CLIP, FAR), over_y(CLIP, NEAR)),
        25: lambda: ring_all(0, ring_s).wait_send(),
        26: lambda: ring_all(1, ring_s).wait_send(),
    }
    for j in range(6, -1, -1):
        for i in range(4):
            for d in (0, 1):
                if i >= 2:
                    send_sum(d, j + 1, LATE[d][i - 2])
                elif j >= 1:
                    send_sum(d, j, AHEAD[d][i])
                else:
                    back(d, 1, AHEAD[d][i]).wait_recv()
            pieces.get((6 - j) * 4 + i, lambda: None)()
    for i in (0, 1):
        for d in (0, 1):
            back(d, 1, LATE[d][i]).wait_recv()
        text_raw(i)
    send_z(CLIP, FAR)
    send_z(CLIP, NEAR)
    hidden_grad(TEXT)
    weight_first(TEXT)
    gathered(TEXT, 1)
    for side in (FAR, NEAR):
        weight(TEXT, side)
    for side in (FAR, NEAR):
        over_y(TEXT, side)
        send_z(TEXT, side)
    over_z(CLIP)
    for d in (0, 1):
        ring_all(d, back_s).wait_send()
    share_emb.wait_send()
    share_grad.wait_send()
    for tower in (CLIP, TEXT):
        hid_all(tower).wait_send()
        relay_all(tower).wait_send()
        ga_both(tower).wait_send()
        yb_both(tower).wait_send()
    zc_all(CLIP).wait_send()
    over_z(TEXT)
    zc_all(TEXT).wait_send()
    fd_all(CLIP).wait()
    fd_all(TEXT).wait()


def hand_over(clip_in, text_in, pieces, clip_hid, text_hid, clip_wg, text_wg, placed, sem):
    copies = [
        pltpu.make_async_copy(clip_in, clip_hid, sem.at[0]),
        pltpu.make_async_copy(text_in, text_hid, sem.at[1]),
        pltpu.make_async_copy(placed.at[CLIP], clip_wg, sem.at[2]),
        pltpu.make_async_copy(placed.at[TEXT], text_wg, sem.at[3]),
    ]
    copies[0].start()
    copies[1].start()
    for tower in (CLIP, TEXT):
        for j in range(16):
            rows, columns = pl.ds(16 * (j // 8), 16), pl.ds(128 * (j % 8), 128)
            placed[tower, rows, columns] = pieces[tower, j].astype(F32)
        copies[2 + tower].start()
    for copy in copies:
        copy.wait()


def local(hv, hc, wv, wc, match, multiplier, offset):
    vmem = pl.BlockSpec(memory_space=pltpu.VMEM)
    anywhere = pl.BlockSpec(memory_space=pl.ANY)
    dma = pltpu.SemaphoreType.DMA
    hidden = jax.ShapeDtypeStruct((TOK, D), BF16)
    gradient = jax.ShapeDtypeStruct((32, E), F32)
    results = pl.pallas_call(
        kernel,
        out_shape=(
            pltpu.VMEM((TOK, D), BF16),
            pltpu.VMEM((TOK, D), BF16),
            pltpu.VMEM((2, 16, 16, 128), BF16),
        ),
        in_specs=[pl.BlockSpec(memory_space=pltpu.HBM)] * 7,
        out_specs=(vmem,) * 3,
        scratch_shapes=[
            pltpu.VMEM((2, D, E), BF16),
            pltpu.VMEM((2, 8, TOK, D), BF16),
            pltpu.VMEM((2, 2, 4, 8, 16, 8 * TOK), BF16),
            pltpu.VMEM((2, TOK, E), F32),
            pltpu.VMEM((2, TOK, 1), F32),
            pltpu.VMEM((9, 2 * TOK, E), BF16),
            pltpu.VMEM((2 * TOK, E), BF16),
            pltpu.VMEM((9, 2 * TOK, E), F32),
            pltpu.VMEM((2 * TOK, E), F32),
            pltpu.VMEM((2, 8, TOK, E), BF16),
            pltpu.VMEM((2, 8, TOK, E), BF16),
            pltpu.VMEM((TOK, E), BF16),
            pltpu.VMEM((TOK, E), BF16),
            pltpu.VMEM((2, TOK, E), BF16),
            pltpu.VMEM((2, 2, 8, HALF, 128), BF16),
            pltpu.VMEM((2, 2, 8, HALF, 128), BF16),
            pltpu.VMEM((2, D // 2, 128), F32),
            pltpu.VMEM((2, 2, 4, 8, 16, 128), BF16),
            pltpu.VMEM((2, 2, 4, 8, 16, 128), BF16),
            pltpu.VMEM((2, NZ, 16, 128), BF16),
            pltpu.VMEM((2, NZ, 16, 128), BF16),
            pltpu.VMEM((32, TOK), jnp.int32),
            pltpu.SMEM((1,), F32),
            pltpu.SMEM((1,), F32),
            dma((7,)),
            dma((2,)),
            dma((2, 8, NC)),
            dma((2,)),
            dma((2, 3, NC)),
            dma((2,)),
            dma((2,)),
            dma((2,)),
            dma((2,)),
            dma((2,)),
            dma((2,)),
            dma((2,)),
            dma((2, 2)),
            dma((2,)),
            dma((2, 2)),
            dma((2,)),
            dma((2,)),
            dma((2,)),
            dma((2,)),
        ],
        compiler_params=pltpu.CompilerParams(
            collective_id=0, has_side_effects=True, vmem_limit_bytes=56 << 20
        ),
    )(hv, hc, wv, wc, match.reshape(32, TOK), multiplier, offset)
    return pl.pallas_call(
        hand_over,
        out_shape=(hidden, hidden, gradient, gradient),
        in_specs=[vmem] * 3,
        out_specs=(anywhere,) * 4,
        scratch_shapes=[pltpu.VMEM((2, 32, E), F32), dma((4,))],
    )(*(pltpu.with_memory_space_constraint(a, pltpu.VMEM) for a in results))


def solution(mesh):
    placed = (P(("grp", "blk"), None), P(("grp", "blk"), None), P(), P(), P("grp"), P(), P())
    return jax.shard_map(
        local,
        mesh=mesh,
        in_specs=placed,
        out_specs=(
            P(("grp", "blk"), None),
            P(("grp", "blk"), None),
            P("blk", None),
            P("blk", None),
        ),
        check_vma=False,
    )
```
